32 devices in a mesh: row: 8 (over y, x, core), col: 4 (over z).
Axes of the slice: x: 2, y: 2, z: 4, core: 2. Of those that a mesh axis runs over, the one named last changes fastest.
Arguments:
- field: bfloat16 [32, 16, 32, 512], P('row', 'col'), may hold values from -6 to 6
- near_kernel: bfloat16 [9, 2, 2, 256, 256], replicated, may hold values from -0.09375 to 0.09375
- contact: int32 [32, 16, 9], P('row', 'col'), may hold values from 0 to 1
- pillar_shift: int32 [32, 16, 2], P('row', 'col'), may hold values from 0 to 15
- wave_index: int32 [2048, 2], replicated, may hold values from -16 to 15
- wave_form: bfloat16 [2048, 2, 256], replicated, may hold values from -0.25 to 0.25
- wave_weight: float32 [2048], replicated, may hold values from 0.5 to 4
Outputs:
- applied: float32 [32, 16, 32, 512], P('row', 'col')
The draws below stay inside these ranges and needn't reach their ends.
All inputs are finite; a program needn't handle non-finite values.
Results may differ from the reference program's by a relative error of at most 0.0038.
Values may be sent and summed in bfloat16 or wider, within the bound.
No kernel may reach another device: no remote copies, remote signals or barrier semaphores. Data moves between devices by JAX's collectives and lax.ppermute only.
A program may use at most 128 MiB of HBM per device.

```python
import math
import jax
import jax.numpy as jnp
from jax import lax

U = 256
W = 2048
S = 32
CLASSES = 2
Q = 16
NRT = 32
NCT = 16


def with_ends(entries, stream_key, smallest, high):
    longest = entries.shape.index(max(entries.shape))
    spots = []
    for shift in (0, 1):
        where = [jax.random.randint(jax.random.fold_in(stream_key, axis), (), 0, length) for axis, length in enumerate(entries.shape)]
        where[longest] = (where[longest] + shift) % entries.shape[longest]
        spots.append(tuple(where))
    return entries.at[spots[0]].set(smallest).at[spots[1]].set(high)


def level_of(stream_key, extent, pieces, least, largest):
    level, own = 1.0, jax.random.fold_in(stream_key, 6)
    for dim, shards_of in pieces:
        heights = jnp.exp(jax.random.uniform(jax.random.fold_in(own, dim), (shards_of,), jnp.float32, least / len(pieces), largest / len(pieces)))
        level = level * jnp.repeat(heights, extent[dim] // shards_of).reshape([-1 if axis == dim else 1 for axis in range(len(extent))])
    return level


def centred(key, shape, width, reach, split=(), held_as=jnp.bfloat16):
    result = width * jax.random.normal(key, shape, jnp.float32)
    if split:
        result = result * level_of(key, shape, split, -0.22, 0.18)
    return jnp.clip(result, -reach, reach).astype(held_as)


def setup_inputs(seed: int = 0) -> dict:
    key_list = jax.random.split(jax.random.key(seed), 8)
    field = centred(key_list[0], (NRT, NCT, S, 2 * U), 1.0, 6.0, ((0, 8), (1, 4)))
    near_kernel = centred(key_list[1], (9, CLASSES, 2, U, U), (18 * U) ** -0.5, 0.09375)
    contact = with_ends(jax.random.randint(key_list[2], (NRT, NCT, 9), 0, CLASSES), jax.random.fold_in(key_list[2], 1), 0, CLASSES - 1).astype(jnp.int32)
    pillar_shift = with_ends(jax.random.randint(key_list[3], (NRT, NCT, 2), 0, Q), jax.random.fold_in(key_list[3], 1), 0, Q - 1).astype(jnp.int32)
    wave_index = with_ends(jax.random.randint(key_list[4], (W, 2), -(NRT // 2), NRT // 2), jax.random.fold_in(key_list[4], 1), -(NRT // 2), (NRT // 2) - 1).astype(jnp.int32)
    wave_form = centred(key_list[5], (W, 2, U), (2 * U) ** -0.5, 0.25)
    wave_weight = jnp.clip(jnp.exp(jax.random.uniform(key_list[6], (W,), jnp.float32, math.log(0.5), math.log(4.0))), 0.5, 4.0)
    return dict(field=field, near_kernel=near_kernel, contact=contact, pillar_shift=pillar_shift, wave_index=wave_index, wave_form=wave_form, wave_weight=wave_weight)


bloch_row = 0.3
bloch_col = 0.17

def realify(real_part, imag_part):
    upper = jnp.concatenate([real_part.T, imag_part.T], axis=1)
    lower = jnp.concatenate([-imag_part.T, real_part.T], axis=1)
    return jnp.concatenate([upper, lower], axis=0)

def wave_angle(wave_index, fine_row, fine_col, row_mod, col_mod):
    order_row = wave_index[:, 0:1]
    order_col = wave_index[:, 1:2]
    turn_row = jnp.mod(order_row * fine_row[None, :], row_mod).astype(jnp.float32) / row_mod
    turn_col = jnp.mod(order_col * fine_col[None, :], col_mod).astype(jnp.float32) / col_mod
    drift = bloch_row * fine_row.astype(jnp.float32) / row_mod + bloch_col * fine_col.astype(jnp.float32) / col_mod
    return 2.0 * math.pi * (turn_row + turn_col + drift[None, :])

def reference(field, near_kernel, contact, pillar_shift, wave_index, wave_form, wave_weight):
    row_mod = Q * NRT
    col_mod = Q * NCT
    wave_matrix = realify(wave_form[:, 0], wave_form[:, 1])
    near_mats = [[realify(near_kernel[offset, variant, 0], near_kernel[offset, variant, 1]) for variant in range(CLASSES)] for offset in range(9)]
    column_ids = jnp.arange(NCT, dtype=jnp.int32)

    def stripe_angles(row_index):
        shifts = lax.dynamic_index_in_dim(pillar_shift, row_index, 0, keepdims=False)
        fine_row = Q * row_index + shifts[:, 0]
        fine_col = Q * column_ids + shifts[:, 1]
        angles = wave_angle(wave_index, fine_row.astype(jnp.int32), fine_col.astype(jnp.int32), row_mod, col_mod)
        return (jnp.cos(angles).T, jnp.sin(angles).T)

    def project(carry, row_index):
        stripe = lax.dynamic_index_in_dim(field, row_index, 0, keepdims=False)
        projected = jnp.dot(stripe.reshape(-1, 2 * U), wave_matrix, preferred_element_type=jnp.float32)
        projected = projected.reshape(NCT, S, 2, W)
        cosine, sine = stripe_angles(row_index)
        hi = lax.Precision.HIGHEST
        coeff_real = jnp.einsum('pw,psw->sw', cosine, projected[:, :, 0], precision=hi) - jnp.einsum('pw,psw->sw', sine, projected[:, :, 1], precision=hi)
        coeff_imag = jnp.einsum('pw,psw->sw', cosine, projected[:, :, 1], precision=hi) + jnp.einsum('pw,psw->sw', sine, projected[:, :, 0], precision=hi)
        return (carry + jnp.stack([coeff_real, coeff_imag], axis=1), None)
    coeff, _ = lax.scan(project, jnp.zeros((S, 2, W), jnp.float32), jnp.arange(NRT, dtype=jnp.int32))
    far_scale = math.sqrt(U / (W * NRT * NCT))
    weighted = ((far_scale * wave_weight)[None, None, :] * coeff).astype(jnp.bfloat16)
    weight_real = weighted[:, 0].astype(jnp.float32)[None]
    weight_imag = weighted[:, 1].astype(jnp.float32)[None]

    def apply_row(row_index):
        near = jnp.zeros((NCT, S, 2 * U), jnp.float32)
        classes = lax.dynamic_index_in_dim(contact, row_index, 0, keepdims=False)
        for offset in range(9):
            step_row = offset // 3 - 1
            step_col = offset % 3 - 1
            source_row = jnp.mod(row_index + step_row, NRT)
            stripe = lax.dynamic_index_in_dim(field, source_row, 0, keepdims=False)
            stripe = jnp.roll(stripe, -step_col, axis=0).reshape(-1, 2 * U)
            for variant in range(CLASSES):
                product = jnp.dot(stripe, near_mats[offset][variant], preferred_element_type=jnp.float32).reshape(NCT, S, 2 * U)
                chosen = (classes[:, offset] == variant)[:, None, None]
                near = near + jnp.where(chosen, product, jnp.float32(0.0))
        cosine, sine = stripe_angles(row_index)
        cos_part = cosine[:, None, :]
        sin_part = sine[:, None, :]
        spread_real = cos_part * weight_real + sin_part * weight_imag
        spread_imag = cos_part * weight_imag - sin_part * weight_real
        spread = jnp.concatenate([spread_real, spread_imag], axis=-1).astype(jnp.bfloat16).reshape(-1, 2 * W)
        far = lax.dot_general(spread, wave_matrix, (((1,), (1,)), ((), ())), preferred_element_type=jnp.float32)
        return near + far.reshape(NCT, S, 2 * U)
    return lax.map(apply_row, jnp.arange(NRT, dtype=jnp.int32))
```

```python
import math

import jax
import jax.numpy as jnp
from jax import lax
from jax.experimental import pallas as pl
from jax.experimental.pallas import tpu as pltpu
from jax.sharding import PartitionSpec as P

Q = 16
LANES = 128

bloch_row = 0.3
bloch_col = 0.17

F32 = jnp.float32
BF16 = jnp.bfloat16
NT = (((1,), (1,)), ((), ()))
HBM = pl.BlockSpec(memory_space=pltpu.MemorySpace.HBM)
VMEM = pl.BlockSpec(memory_space=pltpu.MemorySpace.VMEM)
SMEM = pl.BlockSpec(memory_space=pltpu.MemorySpace.SMEM)


def params(mib):
    return pltpu.CompilerParams(vmem_limit_bytes=mib << 20)


def cost(flops, size):
    return pl.CostEstimate(flops=flops, bytes_accessed=size, transcendentals=0)


def unit(turn):
    y = math.pi * turn
    z = y * y
    even = [(-1) ** k / math.factorial(2 * k) for k in range(8)]
    odd = [(-1) ** k / math.factorial(2 * k + 1) for k in range(8)]
    c = even[7]
    s = odd[7]
    for k in range(6, -1, -1):
        c = c * z + even[k]
        s = s * z + odd[k]
    s = s * y
    return 1.0 - 2.0 * (s * s), 2.0 * (s * c)


def fine(shift, lanes):
    rows, cols = shift.shape[0], shift.shape[2]
    first_row = lax.axis_index("row") * rows
    first_col = lax.axis_index("col") * cols
    spot = lax.broadcasted_iota(jnp.int32, (rows * cols, lanes), 0)
    fr = jnp.zeros(spot.shape, jnp.int32)
    fc = fr
    for p in range(rows * cols):
        r, c = p // cols, p % cols
        fr = jnp.where(spot == p, Q * (first_row + r) + shift[r, 0, c], fr)
        fc = jnp.where(spot == p, Q * (first_col + c) + shift[r, 1, c], fc)
    return fr, fc


def phases(fr, fc, index, row_mod, col_mod):
    turn_row = ((index[0:1] * fr) & (row_mod - 1)).astype(F32) * (1.0 / row_mod)
    turn_col = ((index[1:2] * fc) & (col_mod - 1)).astype(F32) * (1.0 / col_mod)
    drift = (bloch_row / row_mod) * fr.astype(F32) + (bloch_col / col_mod) * fc.astype(F32)
    turn = turn_row + turn_col + drift
    return unit(turn - jnp.round(turn))


def project_body(x_hbm, shift_hbm, index_hbm, weight_hbm, wave_hbm, mine_ref, other_ref, form_ref,
                 xs, left, right, shift, index_ref, weight_ref, g, sem, gsem,
                 *, tile, row_mod, col_mod, scale):
    waves = wave_hbm.shape[0]
    half = waves // 2
    width = wave_hbm.shape[2]
    n = shift.shape[0] * shift.shape[2]
    sources = x_hbm.shape[0] // n
    core = lax.axis_index("row") & 1
    small = [
        pltpu.make_async_copy(src, dst, sem.at[k])
        for k, (src, dst) in enumerate(
            ((x_hbm, xs), (shift_hbm, shift), (index_hbm, index_ref), (weight_hbm, weight_ref))
        )
    ]
    for c in small:
        c.start()
    steps = []
    for t in range(waves // tile):
        flip = 1 if t < waves // tile // 2 else 0
        inside = (t * tile) % half
        first = pl.multiple_of((core ^ flip) * half + inside, tile)
        pair = [
            pltpu.make_async_copy(
                wave_hbm.at[pl.ds(first, tile), :, pl.ds(LANES * j, LANES)], g.at[j, t], gsem.at[t, j]
            )
            for j in range(2)
        ]
        for c in pair:
            c.start()
        steps.append((flip, inside, first, pair))
    a = lax.broadcasted_iota(jnp.int32, (2 * LANES, 2 * LANES), 0)
    b = lax.broadcasted_iota(jnp.int32, (2 * LANES, 2 * LANES), 1)
    sort = jnp.where(b == jnp.where(a < LANES, 2 * a, 2 * (a - LANES) + 1), 1.0, 0.0).astype(BF16)
    for c in small:
        c.wait()
    left[:, :width] = xs[:, :width]
    left[:, width:] = -xs[:, width:]
    right[:, :width] = xs[:, width:]
    right[:, width:] = xs[:, :width]
    fr, fc = fine(shift, tile)
    for t, (flip, inside, first, pair) in enumerate(steps):
        for c in pair:
            c.wait()
        for k in range(tile // LANES):
            at = pl.ds(first + k * LANES, LANES)
            mixed = jnp.concatenate(
                [g[j, t, k * LANES : (k + 1) * LANES].reshape(2 * LANES, LANES) for j in range(2)], axis=1
            )
            d = jnp.dot(sort, mixed, preferred_element_type=F32).astype(BF16)
            form_ref[0, at, :] = d[:LANES]
            form_ref[1, at, :] = d[LANES:]
        at = pl.ds(first, tile)
        w = jnp.concatenate([form_ref[0, at, :], form_ref[1, at, :]], axis=1)
        re = lax.dot_general(left[...], w, NT, preferred_element_type=F32)
        im = lax.dot_general(right[...], w, NT, preferred_element_type=F32)
        cos, sin = phases(fr, fc, index_ref[:, at], row_mod, col_mod)
        ar = jnp.zeros((sources, tile), F32)
        ai = ar
        for p in range(n):
            u = re[p * sources : (p + 1) * sources]
            v = im[p * sources : (p + 1) * sources]
            cp, sp = cos[p : p + 1], sin[p : p + 1]
            ar = ar + (cp * u - sp * v)
            ai = ai + (cp * v + sp * u)
        s = scale * weight_ref[:, at]
        ar = ar * s
        ai = ai * s
        out = other_ref if flip else mine_ref
        for k in range(tile // LANES):
            out[inside // LANES + k, 0] = ar[:, LANES * k : LANES * (k + 1)]
            out[inside // LANES + k, 1] = ai[:, LANES * k : LANES * (k + 1)]


def project(x, shift, index, weight, wave_form, row_mod, col_mod, scale, tile=512):
    waves, _, width = wave_form.shape
    n = shift.shape[0] * shift.shape[2]
    sources = x.shape[0] // n
    half = jax.ShapeDtypeStruct((waves // 2 // LANES, 2, sources, LANES), F32)

    def body(*refs):
        project_body(*refs, tile=tile, row_mod=row_mod, col_mod=col_mod, scale=scale)

    return pl.pallas_call(
        body,
        in_specs=[HBM] * 5,
        out_specs=[VMEM] * 3,
        out_shape=[half, half, jax.ShapeDtypeStruct((2, waves, width), BF16)],
        scratch_shapes=[
            pltpu.VMEM(x.shape, BF16),
            pltpu.VMEM(x.shape, BF16),
            pltpu.VMEM(x.shape, BF16),
            pltpu.SMEM(shift.shape, jnp.int32),
            pltpu.VMEM(index.shape, jnp.int32),
            pltpu.VMEM(weight.shape, F32),
            pltpu.VMEM((2, waves // tile, tile, 2, LANES), BF16),
            pltpu.SemaphoreType.DMA((4,)),
            pltpu.SemaphoreType.DMA((waves // tile, 2)),
        ],
        compiler_params=params(24),
        cost_estimate=cost(8 * x.shape[0] * width * waves, 5 << 20),
        name="project",
    )(x, shift, index, weight, wave_form)


def spread_body(shift_hbm, index_hbm, form_hbm, coeff_ref, base_ref, out_ref, shift, index_ref, form_ref,
                lhs, sem, *, flip, tile, row_mod, col_mod):
    half = form_ref.shape[1]
    width = form_ref.shape[2]
    n = shift.shape[0] * shift.shape[2]
    sources = coeff_ref.shape[2]
    core = (lax.axis_index("row") & 1) ^ flip
    start = pl.multiple_of(core * half, half)
    copies = [
        pltpu.make_async_copy(shift_hbm, shift, sem.at[0]),
        pltpu.make_async_copy(index_hbm.at[:, pl.ds(start, half)], index_ref, sem.at[1]),
        pltpu.make_async_copy(form_hbm.at[:, pl.ds(start, half)], form_ref, sem.at[2]),
    ]
    for c in copies:
        c.start()
    copies[0].wait()
    copies[1].wait()
    fr, fc = fine(shift, tile)
    for t in range(half // tile):
        at = slice(t * tile, (t + 1) * tile)
        cos, sin = phases(fr, fc, index_ref[:, at], row_mod, col_mod)
        groups = range(t * tile // LANES, (t + 1) * tile // LANES)
        wr = jnp.concatenate([coeff_ref[k, 0].astype(F32) for k in groups], axis=1)
        wi = jnp.concatenate([coeff_ref[k, 1].astype(F32) for k in groups], axis=1)
        for p in range(n):
            cp, sp = cos[p : p + 1], sin[p : p + 1]
            sr = (cp * wr + sp * wi).astype(BF16)
            si = (cp * wi - sp * wr).astype(BF16)
            here = slice(p * sources, (p + 1) * sources)
            lhs[0, here, :tile] = sr
            lhs[0, here, tile:] = si
            lhs[1, here, :tile] = si
            lhs[1, here, tile:] = -sr
        if t == 0:
            copies[2].wait()
        w = jnp.concatenate([form_ref[0, at, :], form_ref[1, at, :]], axis=0)
        src = base_ref if t == 0 else out_ref
        for j in range(2):
            cols = slice(j * width, (j + 1) * width)
            out_ref[:, cols] = src[:, cols] + jnp.dot(lhs[j], w, preferred_element_type=F32)


def spread(shift, index, form, coeff, base, row_mod, col_mod, flip, tile=256):
    waves, width = form.shape[1], form.shape[2]

    def body(*refs):
        spread_body(*refs, flip=flip, tile=tile, row_mod=row_mod, col_mod=col_mod)

    return pl.pallas_call(
        body,
        in_specs=[HBM, HBM, HBM, VMEM, VMEM],
        out_specs=VMEM,
        out_shape=jax.ShapeDtypeStruct(base.shape, F32),
        scratch_shapes=[
            pltpu.SMEM(shift.shape, jnp.int32),
            pltpu.VMEM((2, waves // 2), jnp.int32),
            pltpu.VMEM((2, waves // 2, width), BF16),
            pltpu.VMEM((2, base.shape[0], 2 * tile), BF16),
            pltpu.SemaphoreType.DMA((3,)),
        ],
        compiler_params=params(24),
        cost_estimate=cost(2 * base.shape[0] * base.shape[1] * waves, 5 << 20),
        name="spread",
    )(shift, index, form, coeff, base)


def near_body(contact_hbm, x_hbm, north_hbm, south_hbm, west_hbm, east_hbm, kernel_hbm, out_ref,
              contact, x, north, south, west, east, kernel, lhs, sem, ksem):
    rows, cols, sources, full = x.shape
    width = full // 2
    offsets, classes = kernel.shape[0], kernel.shape[1]
    small = [
        pltpu.make_async_copy(src, dst, sem.at[k])
        for k, (src, dst) in enumerate(
            ((contact_hbm, contact), (x_hbm, x), (north_hbm, north), (south_hbm, south),
             (west_hbm, west), (east_hbm, east))
        )
    ]
    for c in small:
        c.start()
    big = [pltpu.make_async_copy(kernel_hbm.at[o], kernel.at[o], ksem.at[o]) for o in range(offsets)]
    for c in big:
        c.start()
    for c in small:
        c.wait()

    def block(r, c):
        if r < 0:
            return north[0, c + 1]
        if r >= rows:
            return south[0, c + 1]
        if c < 0:
            return west[r, 0]
        if c >= cols:
            return east[r, 0]
        return x[r, c]

    for o in range(offsets):
        for p in range(rows * cols):
            r, c = p // cols, p % cols
            here = slice(p * sources, (p + 1) * sources)
            xb = block(r + o // 3 - 1, c + o % 3 - 1)
            for v in range(classes):
                m = jnp.where(contact[r, c, o] == v, xb, jnp.zeros_like(xb))
                lhs[v, here, :full] = m
                lhs[v, here, full:] = -m[:, width:]
        big[o].wait()
        for v in range(classes):
            xr, xi, nx = (lhs[v, :, k * width : (k + 1) * width] for k in range(3))
            w = jnp.concatenate([kernel[o, v, 0], kernel[o, v, 1]], axis=1)
            re = lax.dot_general(jnp.concatenate([xr, nx], axis=1), w, NT, preferred_element_type=F32)
            im = lax.dot_general(jnp.concatenate([xi, xr], axis=1), w, NT, preferred_element_type=F32)
            if o == 0 and v == 0:
                out_ref[:, :width] = re
                out_ref[:, width:] = im
            else:
                out_ref[:, :width] += re
                out_ref[:, width:] += im


def near_field(contact, x, north, south, west, east, kernel):
    rows, cols, sources, full = x.shape
    m = rows * cols * sources
    return pl.pallas_call(
        near_body,
        in_specs=[HBM] * 7,
        out_specs=VMEM,
        out_shape=jax.ShapeDtypeStruct((m, full), F32),
        scratch_shapes=[pltpu.SMEM(contact.shape, jnp.int32)]
        + [pltpu.VMEM(a.shape, BF16) for a in (x, north, south, west, east, kernel)]
        + [
            pltpu.VMEM((kernel.shape[1], m, 3 * full // 2), BF16),
            pltpu.SemaphoreType.DMA((6,)),
            pltpu.SemaphoreType.DMA((kernel.shape[0],)),
        ],
        compiler_params=params(32),
        cost_estimate=cost(2 * kernel.shape[0] * kernel.shape[1] * m * full * full, 8 << 20),
        name="near",
    )(contact, x, north, south, west, east, kernel)


def shifted(cells, axis, step):
    count = lax.axis_size(axis)
    return lax.ppermute(cells, axis, [(i, (i + step) % count) for i in range(count)])


def bits(count, first):
    out = []
    while first < count:
        out.append(first)
        first *= 2
    return out


def exchange(value, dims):
    n_row, n_col = lax.axis_size("row"), lax.axis_size("col")
    pairs = []
    for r in range(n_row):
        for c in range(n_col):
            dr, dc = dims[r & 1]
            pairs.append((r * n_col + c, (r ^ dr) * n_col + (c ^ dc)))
    return lax.ppermute(value, ("row", "col"), pairs)


def local(field, near_kernel, contact, pillar_shift, wave_index, wave_form, wave_weight):
    rows, cols, sources, full = field.shape
    waves = wave_form.shape[0]
    n_row, n_col = lax.axis_size("row"), lax.axis_size("col")
    row_mod = Q * rows * n_row
    col_mod = Q * cols * n_col
    scale = math.sqrt(full // 2 / (waves * rows * n_row * cols * n_col))
    shift = jnp.swapaxes(pillar_shift, 1, 2)
    index = wave_index.T
    weight = wave_weight.reshape(1, -1)
    mine, other, form = project(
        field.reshape(-1, full), shift, index, weight, wave_form, row_mod, col_mod, scale
    )
    total = mine + exchange(other, ((1, 0), (1, 0)))
    by_row = [(b, 0) for b in bits(n_row, 2)]
    by_col = [(0, b) for b in bits(n_col, 1)]
    for dims in zip(by_row + by_col, by_row[::-1] + by_col):
        total = total + exchange(total.astype(jnp.float16), dims).astype(F32)
    weighted = total.astype(BF16)
    weighted_other = exchange(weighted, ((1, 0), (1, 0)))
    west = shifted(field[:, cols - 1 :], "col", 1)
    east = shifted(field[:, :1], "col", -1)
    wide_top = jnp.concatenate([west[:1], field[:1], east[:1]], axis=1)
    wide_bottom = jnp.concatenate([west[-1:], field[-1:], east[-1:]], axis=1)
    north = shifted(wide_bottom, "row", 1)
    south = shifted(wide_top, "row", -1)
    out = near_field(contact, field, north, south, west, east, near_kernel)
    out = spread(shift, index, form, weighted, out, row_mod, col_mod, 0)
    out = spread(shift, index, form, weighted_other, out, row_mod, col_mod, 1)
    return out.reshape(field.shape)


def solution(mesh):
    placed = (
        P("row", "col", None, None),
        P(),
        P("row", "col", None),
        P("row", "col", None),
        P(),
        P(),
        P(),
    )
    return jax.shard_map(
        local, mesh=mesh, in_specs=placed, out_specs=P("row", "col", None, None), check_vma=False
    )
```

```python
import math

import jax
import jax.numpy as jnp
from jax import lax
from jax.experimental import pallas as pl
from jax.experimental.pallas import tpu as pltpu
from jax.sharding import PartitionSpec as P

Q = 16
LANES = 128
TILE = 256

bloch_row = 0.3
bloch_col = 0.17

F32 = jnp.float32
BF16 = jnp.bfloat16
NT = (((1,), (1,)), ((), ()))
HBM = pl.BlockSpec(memory_space=pltpu.MemorySpace.HBM)
VMEM = pl.BlockSpec(memory_space=pltpu.MemorySpace.VMEM)
SMEM = pl.BlockSpec(memory_space=pltpu.MemorySpace.SMEM)


def params(mib):
    return pltpu.CompilerParams(vmem_limit_bytes=mib << 20)


def cost(flops, size):
    return pl.CostEstimate(flops=flops, bytes_accessed=size, transcendentals=0)


def unit(turn):
    y = math.pi * turn
    z = y * y
    even = [(-1) ** k / math.factorial(2 * k) for k in range(8)]
    odd = [(-1) ** k / math.factorial(2 * k + 1) for k in range(8)]
    c = even[7]
    s = odd[7]
    for k in range(6, -1, -1):
        c = c * z + even[k]
        s = s * z + odd[k]
    s = s * y
    return 1.0 - 2.0 * (s * s), 2.0 * (s * c)


def fine(shift, lanes):
    rows, cols = shift.shape[0], shift.shape[2]
    first_row = lax.axis_index("row") * rows
    first_col = lax.axis_index("col") * cols
    spot = lax.broadcasted_iota(jnp.int32, (rows * cols, lanes), 0)
    fr = jnp.zeros(spot.shape, jnp.int32)
    fc = fr
    for p in range(rows * cols):
        r, c = p // cols, p % cols
        fr = jnp.where(spot == p, Q * (first_row + r) + shift[r, 0, c], fr)
        fc = jnp.where(spot == p, Q * (first_col + c) + shift[r, 1, c], fc)
    return fr, fc


def phases(fr, fc, index, row_mod, col_mod):
    turn_row = ((index[0:1] * fr) & (row_mod - 1)).astype(F32) * (1.0 / row_mod)
    turn_col = ((index[1:2] * fc) & (col_mod - 1)).astype(F32) * (1.0 / col_mod)
    drift = (bloch_row / row_mod) * fr.astype(F32) + (bloch_col / col_mod) * fc.astype(F32)
    turn = turn_row + turn_col + drift
    return unit(turn - jnp.round(turn))


def real_form(form, first, tile):
    re = form[0, first : first + tile, :]
    im = form[1, first : first + tile, :]
    upper = jnp.concatenate([re, -im], axis=1)
    lower = jnp.concatenate([im, re], axis=1)
    return jnp.concatenate([upper, lower], axis=0)


def project_body(x_hbm, shift_hbm, index_hbm, weight_hbm, contact_hbm, wave_hbm, kernel_hbm,
                 mine_ref, other_ref, mine_hbm, other_hbm, trig_ref, xs, mask_ref, middle_ref, sides_ref,
                 form_mine, form_other, form_sem, both, contact, shift, index_ref, weight_ref, g, sem, gsem,
                 *, tile, row_mod, col_mod, scale):
    waves = wave_hbm.shape[0]
    half = waves // 2
    width = wave_hbm.shape[2]
    n = shift.shape[0] * shift.shape[2]
    sources = x_hbm.shape[0] // n
    core = lax.axis_index("row") & 1
    small = [
        pltpu.make_async_copy(src, dst, sem.at[k])
        for k, (src, dst) in enumerate(
            (
                (shift_hbm, shift), (index_hbm, index_ref), (weight_hbm, weight_ref), (x_hbm, xs),
                (contact_hbm, contact), (kernel_hbm.at[4], middle_ref.at[0]),
                (kernel_hbm.at[3], sides_ref.at[0]), (kernel_hbm.at[5], sides_ref.at[1]),
            )
        )
    ]
    for c in small[:4]:
        c.start()
    steps = []
    for t in range(waves // tile):
        flip = 1 if t < waves // tile // 2 else 0
        inside = (t * tile) % half
        first = pl.multiple_of((core ^ flip) * half + inside, tile)
        pair = [pltpu.make_async_copy(wave_hbm.at[pl.ds(first, tile)], g.at[t], gsem.at[t])]
        for c in pair:
            c.start()
        steps.append((flip, inside, first, pair))
    for c in small[4:]:
        c.start()
    a = lax.broadcasted_iota(jnp.int32, (2 * LANES, 2 * LANES), 0)
    b = lax.broadcasted_iota(jnp.int32, (2 * LANES, 2 * LANES), 1)
    sort = jnp.where(b == jnp.where(a < LANES, 2 * a, 2 * (a - LANES) + 1), 1.0, 0.0).astype(BF16)
    for c in small[:3]:
        c.wait()
    fr, fc = fine(shift, tile)
    def unmix(t):
        flip, inside, first, pair = steps[t]
        if t == 0:
            pair[0].wait()
        if t == 1:
            for step in steps[1:]:
                step[3][0].wait()
        form = form_other if flip else form_mine
        for k in range(tile // LANES):
            mixed = g[t, k * LANES : (k + 1) * LANES].reshape(2 * LANES, width)
            d = jnp.dot(sort, mixed, preferred_element_type=F32).astype(BF16)
            at = slice(inside + k * LANES, inside + (k + 1) * LANES)
            form[0, at, :] = d[:LANES]
            form[1, at, :] = d[LANES:]

        copies = [
            pltpu.make_async_copy(
                form.at[k, pl.ds(inside, tile)],
                (other_hbm if flip else mine_hbm).at[k, pl.ds(inside, tile)],
                form_sem.at[t, k],
            )
            for k in range(2)
        ]
        for c in copies:
            c.start()
        return copies

    def multiply(t):
        flip, inside, first, pair = steps[t]
        form = form_other if flip else form_mine
        both[t % 2] = lax.dot_general(xs[...], real_form(form, inside, tile), NT, preferred_element_type=F32)

    def angles(t):
        flip, inside, first, pair = steps[t]
        at = pl.ds(first, tile)
        cos, sin = phases(fr, fc, index_ref[:, at], row_mod, col_mod)
        trig_ref[0, :, at] = cos
        trig_ref[1, :, at] = sin

    def add(t):
        flip, inside, first, pair = steps[t]
        at = pl.ds(first, tile)
        ar = jnp.zeros((sources, tile), F32)
        ai = ar
        for p in range(n):
            here = slice(p * sources, (p + 1) * sources)
            u, v = both[t % 2, here, :tile], both[t % 2, here, tile:]
            cp, sp = trig_ref[0, p : p + 1, at], trig_ref[1, p : p + 1, at]
            ar = ar + (cp * u - sp * v)
            ai = ai + (cp * v + sp * u)
        s = scale * weight_ref[:, at]
        ar = ar * s
        ai = ai * s
        out = other_ref if flip else mine_ref
        for k in range(tile // LANES):
            out[inside // LANES + k, 0] = ar[:, LANES * k : LANES * (k + 1)]
            out[inside // LANES + k, 1] = ai[:, LANES * k : LANES * (k + 1)]

    count = len(steps)
    angles(0)
    stores = unmix(0)
    small[3].wait()
    for t in range(count):
        if t + 1 < count:
            stores += unmix(t + 1)
        multiply(t)
        if t + 1 < count:
            angles(t + 1)
        if t > 0:
            add(t - 1)
    add(count - 1)
    for c in small[4:] + stores:
        c.wait()
    cols = shift.shape[2]
    for o in range(mask_ref.shape[0]):
        for p in range(n):
            chosen = jnp.full((1, LANES), contact[p // cols, p % cols, o], jnp.int32)
            mask_ref[o, p : p + 1, :] = chosen.astype(F32)


def in_hbm(*arrays):
    return [pltpu.with_memory_space_constraint(a, pltpu.MemorySpace.HBM) for a in arrays]


def project(x, shift, index, weight, contact, wave_form, near_kernel, row_mod, col_mod, scale, tile=TILE):
    waves, _, width = wave_form.shape
    n = shift.shape[0] * shift.shape[2]
    sources = x.shape[0] // n
    half = pltpu.VMEM((waves // 2 // LANES, 2, sources, LANES), F32)

    form = pltpu.HBM((2, waves // 2, width), BF16)

    def body(*refs):
        project_body(*refs, tile=tile, row_mod=row_mod, col_mod=col_mod, scale=scale)

    return pl.pallas_call(
        body,
        in_specs=[HBM] * 7,
        out_specs=[VMEM] * 2 + [HBM] * 2 + [VMEM] * 5,
        out_shape=[
            half,
            half,
            form,
            form,
            pltpu.VMEM((2, n, waves), F32),
            pltpu.VMEM(x.shape, BF16),
            pltpu.VMEM((contact.shape[2], n, LANES), F32),
            pltpu.VMEM((1,) + near_kernel.shape[1:], BF16),
            pltpu.VMEM((2,) + near_kernel.shape[1:], BF16),
        ],
        scratch_shapes=[
            pltpu.VMEM((2, waves // 2, width), BF16),
            pltpu.VMEM((2, waves // 2, width), BF16),
            pltpu.SemaphoreType.DMA((waves // tile, 2)),
            pltpu.VMEM((2, x.shape[0], 2 * tile), F32),
            pltpu.SMEM(contact.shape, jnp.int32),
            pltpu.SMEM(shift.shape, jnp.int32),
            pltpu.VMEM(index.shape, jnp.int32),
            pltpu.VMEM(weight.shape, F32),
            pltpu.VMEM((waves // tile, tile, 2, width), BF16),
            pltpu.SemaphoreType.DMA((8,)),
            pltpu.SemaphoreType.DMA((waves // tile,)),
        ],
        compiler_params=params(24),
        cost_estimate=cost(8 * x.shape[0] * width * waves, 5 << 20),
        name="project",
    )(*in_hbm(x, shift, index, weight, contact, wave_form, near_kernel))


def spread_body(trig_ref, form_ref, coeff_ref, base_ref, out_ref, lhs, *, flip, tile):
    waves = trig_ref.shape[2]
    half = waves // 2
    n = trig_ref.shape[1]
    sources = coeff_ref.shape[2]
    core = (lax.axis_index("row") & 1) ^ flip
    for t in range(half // tile):
        at = pl.ds(pl.multiple_of(core * half + t * tile, tile), tile)
        cos, sin = trig_ref[0, :, at], trig_ref[1, :, at]
        groups = range(t * tile // LANES, (t + 1) * tile // LANES)
        wr = jnp.concatenate([coeff_ref[k, 0].astype(F32) for k in groups], axis=1)
        wi = jnp.concatenate([coeff_ref[k, 1].astype(F32) for k in groups], axis=1)
        for p in range(n):
            cp, sp = cos[p : p + 1], sin[p : p + 1]
            here = slice(p * sources, (p + 1) * sources)
            lhs[t, here, :tile] = (cp * wr + sp * wi).astype(BF16)
            lhs[t, here, tile:] = (cp * wi - sp * wr).astype(BF16)
        src = base_ref if t == 0 else out_ref
        w = real_form(form_ref, t * tile, tile)
        out_ref[...] = src[...] + jnp.dot(lhs[t], w, preferred_element_type=F32)


def spread(trig, form, coeff, base, flip, tile=TILE):
    half = trig.shape[2] // 2

    def body(*refs):
        spread_body(*refs, flip=flip, tile=tile)

    return pl.pallas_call(
        body,
        in_specs=[VMEM] * 4,
        out_specs=VMEM,
        out_shape=jax.ShapeDtypeStruct(base.shape, F32),
        scratch_shapes=[pltpu.VMEM((half // tile, base.shape[0], 2 * tile), BF16)],
        compiler_params=params(24),
        cost_estimate=cost(4 * base.shape[0] * base.shape[1] * half, 5 << 20),
        name="spread",
    )(trig, form, coeff, base)


def near_body(*refs, offsets, coming, halo, after):
    mask_ref, x = refs[:2]
    halos = refs[2 : 2 + halo]
    held, refs = refs[2 + halo], refs[3 + halo :]
    if coming:
        kernel_hbm, refs = refs[0], refs[1:]
    if after:
        base_ref, refs = refs[0], refs[1:]
    out_ref, refs = refs[0], refs[1:]
    copies = []
    if coming:
        copies = [
            pltpu.make_async_copy(kernel_hbm.at[o], refs[0].at[k], refs[2].at[k]) for k, o in enumerate(coming)
        ]
        for c in copies:
            c.start()
        refs = refs[1:]
    lhs = refs[0]
    rows, cols, sources, full = x.shape
    classes = held.shape[1]

    def block(r, c):
        if r < 0:
            return halos[2][0, c + 1]
        if r >= rows:
            return halos[3][0, c + 1]
        if c < 0:
            return halos[0][r, 0]
        if c >= cols:
            return halos[1][r, 0]
        return x[r, c]

    def gather(k):
        o = offsets[k]
        for p in range(rows * cols):
            r, c = p // cols, p % cols
            here = slice(p * sources, (p + 1) * sources)
            xb = block(r + o // 3 - 1, c + o % 3 - 1)
            m = jnp.broadcast_to(mask_ref[o, p : p + 1, :], (sources, LANES)).astype(BF16)
            second = xb * jnp.concatenate([m] * (full // LANES), axis=1)
            lhs[k % 2, here, :full] = xb - second
            lhs[k % 2, here, full:] = second

    for k, o in enumerate(offsets):
        gather(k)
        upper, lower = [], []
        for v in range(classes):
            re, im = held[k, v, 0], held[k, v, 1]
            upper += [re, -im]
            lower += [im, re]
        w = jnp.concatenate([jnp.concatenate(upper, axis=1), jnp.concatenate(lower, axis=1)], axis=0)
        product = lax.dot_general(lhs[k % 2], w, NT, preferred_element_type=F32)
        if k == 0 and not after:
            out_ref[...] = product
        else:
            out_ref[...] = (base_ref if k == 0 else out_ref)[...] + product


    for c in copies:
        c.wait()


def near_field(offsets, coming, mask, x, halos, held, kernel, base=None):
    rows, cols, sources, full = x.shape
    m = rows * cols * sources
    classes = kernel.shape[1]
    after = base is not None

    def body(*refs):
        near_body(*refs, offsets=offsets, coming=coming, halo=len(halos), after=after)

    operands = [mask, x, *halos, held]
    specs = [VMEM] * len(operands)
    out = [pltpu.VMEM((m, full), F32)]
    scratch = [pltpu.VMEM((2, m, classes * full), BF16)]
    if coming:
        operands += in_hbm(kernel)
        specs += [HBM]
        out += [pltpu.VMEM((len(coming),) + kernel.shape[1:], BF16)]
        scratch += [pltpu.SemaphoreType.DMA((len(coming),))]
    return pl.pallas_call(
        body,
        in_specs=specs + [VMEM] * after,
        out_specs=[VMEM] * len(out),
        out_shape=out,
        scratch_shapes=scratch,
        compiler_params=params(24),
        cost_estimate=cost(2 * len(offsets) * classes * m * full * full, 4 << 20),
        name="near",
    )(*operands, *[base] * after)


def paired(low, high, axis):
    count = lax.axis_size(axis)
    odd = (lax.axis_index(axis) & 1) == 1
    inner = [(i, i ^ 1) for i in range(count)]
    outer = [(i, (i + 1 if i & 1 else i - 1) % count) for i in range(count)]

    def first():
        return lax.ppermute(jnp.where(odd, low, high), axis, inner)

    def second():
        return lax.ppermute(jnp.where(odd, high, low), axis, outer)

    def sort(a, b):
        return jnp.where(odd, a, b), jnp.where(odd, b, a)

    return first, second, sort


def bits(count, first):
    out = []
    while first < count:
        out.append(first)
        first *= 2
    return out


def exchange(value, dims):
    n_row, n_col = lax.axis_size("row"), lax.axis_size("col")
    pairs = []
    for r in range(n_row):
        for c in range(n_col):
            dr, dc = dims[r & 1]
            pairs.append((r * n_col + c, (r ^ dr) * n_col + (c ^ dc)))
    return lax.ppermute(value, ("row", "col"), pairs)


def pack(value):
    return (value * (128.0 * lax.rsqrt(jnp.maximum(jnp.abs(value), 1e-36)))).astype(jnp.float16)


def unpack(got):
    root = got.astype(F32)
    return root * jnp.abs(root) * (1.0 / 128.0**2)


def local(field, near_kernel, contact, pillar_shift, wave_index, wave_form, wave_weight):
    rows, cols, sources, full = field.shape
    waves = wave_form.shape[0]
    n_row, n_col = lax.axis_size("row"), lax.axis_size("col")
    row_mod = Q * rows * n_row
    col_mod = Q * cols * n_col
    scale = math.sqrt(full // 2 / (waves * rows * n_row * cols * n_col))
    shift = jnp.swapaxes(pillar_shift, 1, 2)
    index = wave_index.T
    weight = wave_weight.reshape(1, -1)
    mine, other, form, form_other, trig, cells, mask, middle, sides = project(
        field.reshape(-1, full), shift, index, weight, contact, wave_form, near_kernel, row_mod, col_mod, scale
    )
    cells = cells.reshape(field.shape)
    total = mine + exchange(other, ((1, 0), (1, 0)))
    by_row = [(b, 0) for b in bits(n_row, 2)]
    by_col = [(0, b) for b in bits(n_col, 1)]
    steps = list(zip(by_row + by_col, by_row[::-1] + by_col[::-1]))
    tie = lax.optimization_barrier

    payload, here = tie((pack(total), cells))
    got = exchange(payload, steps[0])
    _, second, _ = paired(here[:, :1], here[:, cols - 1 :], "col")
    outer = second()
    total = total + unpack(got)

    payload, here = tie((pack(total), here))
    got = exchange(payload, steps[1])
    first, _, sort = paired(here[:, :1], here[:, cols - 1 :], "col")
    inner = first()
    out, upper = near_field((4,), (0, 1, 2), mask, here, (), middle, near_kernel)
    total = total + unpack(got)

    west, east = sort(inner, outer)
    payload, out = tie((pack(total), out))
    got = exchange(payload, steps[2])
    low = jnp.concatenate([west[:1], cells[:1], east[:1]], axis=1)
    high = jnp.concatenate([west[-1:], cells[-1:], east[-1:]], axis=1)
    first, second, sort = paired(low, high, "row")
    north, south = sort(first(), second())
    out, lower = near_field((3, 5), (6, 7, 8), mask, cells, (west, east), sides, near_kernel, out)
    total = total + unpack(got)

    payload, out = tie((pack(total), out))
    got = exchange(payload, steps[3])
    halos = (west, east, north, south)
    (out,) = near_field((0, 1, 2), (), mask, cells, halos, upper, near_kernel, out)
    (out,) = near_field((6, 7, 8), (), mask, cells, halos, lower, near_kernel, out)
    total = total + unpack(got)
    for dims in steps[4:]:
        total = total + unpack(exchange(pack(total), dims))
    weighted, out = tie((total.astype(BF16), out))
    weighted_other = exchange(weighted, ((1, 0), (1, 0)))
    out = spread(trig, form, weighted, out, 0)
    out = spread(trig, form_other, weighted_other, out, 1)
    return out.reshape(field.shape)


def solution(mesh):
    placed = (
        P("row", "col", None, None),
        P(),
        P("row", "col", None),
        P("row", "col", None),
        P(),
        P(),
        P(),
    )
    return jax.shard_map(
        local, mesh=mesh, in_specs=placed, out_specs=P("row", "col", None, None), check_vma=False
    )
```

```python
import math

import jax
import jax.numpy as jnp
from jax import lax
from jax.experimental import pallas as pl
from jax.experimental.pallas import tpu as pltpu
from jax.sharding import PartitionSpec as P

Q = 16
LANES = 128
TILE = 256

bloch_row = 0.3
bloch_col = 0.17

F32 = jnp.float32
BF16 = jnp.bfloat16
NT = (((1,), (1,)), ((), ()))
HBM = pl.BlockSpec(memory_space=pltpu.MemorySpace.HBM)
VMEM = pl.BlockSpec(memory_space=pltpu.MemorySpace.VMEM)
SMEM = pl.BlockSpec(memory_space=pltpu.MemorySpace.SMEM)


def params(mib):
    return pltpu.CompilerParams(vmem_limit_bytes=mib << 20)


def cost(flops, size):
    return pl.CostEstimate(flops=flops, bytes_accessed=size, transcendentals=0)


def unit(turn):
    y = math.pi * turn
    z = y * y
    even = [(-1) ** k / math.factorial(2 * k) for k in range(8)]
    odd = [(-1) ** k / math.factorial(2 * k + 1) for k in range(8)]
    c = even[7]
    s = odd[7]
    for k in range(6, -1, -1):
        c = c * z + even[k]
        s = s * z + odd[k]
    s = s * y
    return 1.0 - 2.0 * (s * s), 2.0 * (s * c)


def fine(shift, lanes):
    rows, cols = shift.shape[0], shift.shape[2]
    first_row = lax.axis_index("row") * rows
    first_col = lax.axis_index("col") * cols
    spot = lax.broadcasted_iota(jnp.int32, (rows * cols, lanes), 0)
    fr = jnp.zeros(spot.shape, jnp.int32)
    fc = fr
    for p in range(rows * cols):
        r, c = p // cols, p % cols
        fr = jnp.where(spot == p, Q * (first_row + r) + shift[r, 0, c], fr)
        fc = jnp.where(spot == p, Q * (first_col + c) + shift[r, 1, c], fc)
    return fr, fc


def phases(fr, fc, index, row_mod, col_mod):
    turn_row = ((index[0:1] * fr) & (row_mod - 1)).astype(F32) * (1.0 / row_mod)
    turn_col = ((index[1:2] * fc) & (col_mod - 1)).astype(F32) * (1.0 / col_mod)
    drift = (bloch_row / row_mod) * fr.astype(F32) + (bloch_col / col_mod) * fc.astype(F32)
    turn = turn_row + turn_col + drift
    return unit(turn - jnp.round(turn))


def real_form(form, first, tile):
    re = form[0, first : first + tile, :]
    im = form[1, first : first + tile, :]
    upper = jnp.concatenate([re, -im], axis=1)
    lower = jnp.concatenate([im, re], axis=1)
    return jnp.concatenate([upper, lower], axis=0)


def project_body(x_hbm, shift_hbm, index_hbm, weight_hbm, contact_hbm, wave_hbm,
                 mine_ref, other_ref, form_mine, form_other, trig_ref, xs, mask_ref,
                 both, contact, shift, index_ref, weight_ref, g, sem, gsem,
                 *, tile, row_mod, col_mod, scale):
    waves = wave_hbm.shape[0]
    half = waves // 2
    width = wave_hbm.shape[2]
    n = shift.shape[0] * shift.shape[2]
    sources = x_hbm.shape[0] // n
    core = lax.axis_index("row") & 1
    small = [
        pltpu.make_async_copy(src, dst, sem.at[k])
        for k, (src, dst) in enumerate(
            (
                (shift_hbm, shift), (index_hbm, index_ref), (weight_hbm, weight_ref), (x_hbm, xs),
                (contact_hbm, contact),
            )
        )
    ]
    for c in small[:4]:
        c.start()
    steps = []
    for t in range(waves // tile):
        flip = 1 if t < waves // tile // 2 else 0
        inside = (t * tile) % half
        first = pl.multiple_of((core ^ flip) * half + inside, tile)
        pair = [pltpu.make_async_copy(wave_hbm.at[pl.ds(first, tile)], g.at[t], gsem.at[t])]
        for c in pair:
            c.start()
        steps.append((flip, inside, first, pair))
    for c in small[4:]:
        c.start()
    a = lax.broadcasted_iota(jnp.int32, (2 * LANES, 2 * LANES), 0)
    b = lax.broadcasted_iota(jnp.int32, (2 * LANES, 2 * LANES), 1)
    sort = jnp.where(b == jnp.where(a < LANES, 2 * a, 2 * (a - LANES) + 1), 1.0, 0.0).astype(BF16)
    for c in small[:3]:
        c.wait()
    fr, fc = fine(shift, tile)
    def unmix(t):
        flip, inside, first, pair = steps[t]
        if t == 0:
            pair[0].wait()
        if t == 1:
            for step in steps[1:]:
                step[3][0].wait()
        form = form_other if flip else form_mine
        for k in range(tile // LANES):
            mixed = g[t, k * LANES : (k + 1) * LANES].reshape(2 * LANES, width)
            d = jnp.dot(sort, mixed, preferred_element_type=F32).astype(BF16)
            at = slice(inside + k * LANES, inside + (k + 1) * LANES)
            form[0, at, :] = d[:LANES]
            form[1, at, :] = d[LANES:]

    def multiply(t):
        flip, inside, first, pair = steps[t]
        form = form_other if flip else form_mine
        both[t % 2] = lax.dot_general(xs[...], real_form(form, inside, tile), NT, preferred_element_type=F32)

    def angles(t):
        flip, inside, first, pair = steps[t]
        at = pl.ds(first, tile)
        cos, sin = phases(fr, fc, index_ref[:, at], row_mod, col_mod)
        trig_ref[0, :, at] = cos
        trig_ref[1, :, at] = sin

    def add(t):
        flip, inside, first, pair = steps[t]
        at = pl.ds(first, tile)
        ar = jnp.zeros((sources, tile), F32)
        ai = ar
        for p in range(n):
            here = slice(p * sources, (p + 1) * sources)
            u, v = both[t % 2, here, :tile], both[t % 2, here, tile:]
            cp, sp = trig_ref[0, p : p + 1, at], trig_ref[1, p : p + 1, at]
            ar = ar + (cp * u - sp * v)
            ai = ai + (cp * v + sp * u)
        s = scale * weight_ref[:, at]
        ar = ar * s
        ai = ai * s
        out = other_ref if flip else mine_ref
        for k in range(tile // LANES):
            out[inside // LANES + k, 0] = ar[:, LANES * k : LANES * (k + 1)]
            out[inside // LANES + k, 1] = ai[:, LANES * k : LANES * (k + 1)]

    count = len(steps)
    angles(0)
    unmix(0)
    small[3].wait()
    for t in range(count):
        if t + 1 < count:
            unmix(t + 1)
        multiply(t)
        if t + 1 < count:
            angles(t + 1)
        if t > 0:
            add(t - 1)
    add(count - 1)
    for c in small[4:]:
        c.wait()
    cols = shift.shape[2]
    for o in range(mask_ref.shape[0]):
        for p in range(n):
            chosen = jnp.full((1, LANES), contact[p // cols, p % cols, o], jnp.int32)
            mask_ref[o, p : p + 1, :] = chosen.astype(F32)


def in_hbm(*arrays):
    return [pltpu.with_memory_space_constraint(a, pltpu.MemorySpace.HBM) for a in arrays]


def project(x, shift, index, weight, contact, wave_form, row_mod, col_mod, scale, tile=TILE):
    waves, _, width = wave_form.shape
    n = shift.shape[0] * shift.shape[2]
    sources = x.shape[0] // n
    half = pltpu.VMEM((waves // 2 // LANES, 2, sources, LANES), F32)

    form = pltpu.VMEM((2, waves // 2, width), BF16)

    def body(*refs):
        project_body(*refs, tile=tile, row_mod=row_mod, col_mod=col_mod, scale=scale)

    return pl.pallas_call(
        body,
        in_specs=[HBM] * 6,
        out_specs=[VMEM] * 7,
        out_shape=[
            half,
            half,
            form,
            form,
            pltpu.VMEM((2, n, waves), F32),
            pltpu.VMEM(x.shape, BF16),
            pltpu.VMEM((contact.shape[2], n, LANES), F32),
        ],
        scratch_shapes=[
            pltpu.VMEM((2, x.shape[0], 2 * tile), F32),
            pltpu.SMEM(contact.shape, jnp.int32),
            pltpu.SMEM(shift.shape, jnp.int32),
            pltpu.VMEM(index.shape, jnp.int32),
            pltpu.VMEM(weight.shape, F32),
            pltpu.VMEM((waves // tile, tile, 2, width), BF16),
            pltpu.SemaphoreType.DMA((8,)),
            pltpu.SemaphoreType.DMA((waves // tile,)),
        ],
        compiler_params=params(24),
        cost_estimate=cost(8 * x.shape[0] * width * waves, 5 << 20),
        name="project",
    )(*in_hbm(x, shift, index, weight, contact, wave_form))


def spread_body(trig_ref, form_ref, coeff_ref, base_ref, out_ref, lhs, *, flip, tile):
    waves = trig_ref.shape[2]
    half = waves // 2
    n = trig_ref.shape[1]
    sources = coeff_ref.shape[2]
    core = (lax.axis_index("row") & 1) ^ flip
    for t in range(half // tile):
        at = pl.ds(pl.multiple_of(core * half + t * tile, tile), tile)
        cos, sin = trig_ref[0, :, at], trig_ref[1, :, at]
        groups = range(t * tile // LANES, (t + 1) * tile // LANES)
        wr = jnp.concatenate([coeff_ref[k, 0].astype(F32) for k in groups], axis=1)
        wi = jnp.concatenate([coeff_ref[k, 1].astype(F32) for k in groups], axis=1)
        for p in range(n):
            cp, sp = cos[p : p + 1], sin[p : p + 1]
            here = slice(p * sources, (p + 1) * sources)
            lhs[t, here, :tile] = (cp * wr + sp * wi).astype(BF16)
            lhs[t, here, tile:] = (cp * wi - sp * wr).astype(BF16)
        src = base_ref if t == 0 else out_ref
        w = real_form(form_ref, t * tile, tile)
        out_ref[...] = src[...] + jnp.dot(lhs[t], w, preferred_element_type=F32)


def spread(trig, form, coeff, base, flip, tile=TILE):
    half = trig.shape[2] // 2

    def body(*refs):
        spread_body(*refs, flip=flip, tile=tile)

    return pl.pallas_call(
        body,
        in_specs=[VMEM] * 4,
        out_specs=VMEM,
        out_shape=jax.ShapeDtypeStruct(base.shape, F32),
        scratch_shapes=[pltpu.VMEM((half // tile, base.shape[0], 2 * tile), BF16)],
        compiler_params=params(24),
        cost_estimate=cost(4 * base.shape[0] * base.shape[1] * half, 5 << 20),
        name="spread",
    )(trig, form, coeff, base)


def near_body(*refs, offsets, coming, halo, given, after):
    mask_ref, x = refs[:2]
    halos = refs[2 : 2 + halo]
    refs = refs[2 + halo :]
    if given:
        held, refs = refs[0], refs[1:]
    if coming:
        kernel_hbm, refs = refs[0], refs[1:]
    if after:
        base_ref, refs = refs[0], refs[1:]
    out_ref, refs = refs[0], refs[1:]
    copies = []
    if coming:
        copies = [
            pltpu.make_async_copy(kernel_hbm.at[o], refs[0].at[k], refs[2].at[k]) for k, o in enumerate(coming)
        ]
        refs = refs[1:]
    lhs = refs[0]
    if not given:
        held = refs[2]
        own = pltpu.make_async_copy(kernel_hbm.at[offsets[0]], held.at[0], refs[3])
        own.start()
    for c in copies:
        c.start()
    rows, cols, sources, full = x.shape
    classes = 2

    def block(r, c):
        if r < 0:
            return halos[2][0, c + 1]
        if r >= rows:
            return halos[3][0, c + 1]
        if c < 0:
            return halos[0][r, 0]
        if c >= cols:
            return halos[1][r, 0]
        return x[r, c]

    def gather(k):
        o = offsets[k]
        for p in range(rows * cols):
            r, c = p // cols, p % cols
            here = slice(p * sources, (p + 1) * sources)
            xb = block(r + o // 3 - 1, c + o % 3 - 1)
            m = jnp.broadcast_to(mask_ref[o, p : p + 1, :], (sources, LANES)).astype(BF16)
            second = xb * jnp.concatenate([m] * (full // LANES), axis=1)
            lhs[k % 2, here, :full] = xb - second
            lhs[k % 2, here, full:] = second

    for k, o in enumerate(offsets):
        gather(k)
        if not given:
            own.wait()
        upper, lower = [], []
        for v in range(classes):
            re, im = held[k, v, 0], held[k, v, 1]
            upper += [re, -im]
            lower += [im, re]
        w = jnp.concatenate([jnp.concatenate(upper, axis=1), jnp.concatenate(lower, axis=1)], axis=0)
        product = lax.dot_general(lhs[k % 2], w, NT, preferred_element_type=F32)
        if k == 0 and not after:
            out_ref[...] = product
        else:
            out_ref[...] = (base_ref if k == 0 else out_ref)[...] + product


    for c in copies:
        c.wait()


def near_field(offsets, coming, mask, x, halos, held, kernel, base=None):
    rows, cols, sources, full = x.shape
    m = rows * cols * sources
    classes = kernel.shape[1]
    after = base is not None

    def body(*refs):
        near_body(*refs, offsets=offsets, coming=coming, halo=len(halos), given=held is not None, after=after)

    operands = [mask, x, *halos] + ([] if held is None else [held])
    specs = [VMEM] * len(operands)
    out = [pltpu.VMEM((m, full), F32)]
    scratch = [pltpu.VMEM((2, m, classes * full), BF16)]
    if coming:
        operands += in_hbm(kernel)
        specs += [HBM]
        out += [pltpu.VMEM((len(coming),) + kernel.shape[1:], BF16)]
        scratch += [pltpu.SemaphoreType.DMA((len(coming),))]
    if held is None:
        scratch += [pltpu.VMEM((1,) + kernel.shape[1:], BF16), pltpu.SemaphoreType.DMA(())]
    return pl.pallas_call(
        body,
        in_specs=specs + [VMEM] * after,
        out_specs=[VMEM] * len(out),
        out_shape=out,
        scratch_shapes=scratch,
        compiler_params=params(24),
        cost_estimate=cost(2 * len(offsets) * classes * m * full * full, 4 << 20),
        name="near",
    )(*operands, *[base] * after)


def paired(low, high, axis):
    count = lax.axis_size(axis)
    odd = (lax.axis_index(axis) & 1) == 1
    inner = [(i, i ^ 1) for i in range(count)]
    outer = [(i, (i + 1 if i & 1 else i - 1) % count) for i in range(count)]

    def first():
        return lax.ppermute(jnp.where(odd, low, high), axis, inner)

    def second():
        return lax.ppermute(jnp.where(odd, high, low), axis, outer)

    def sort(a, b):
        return jnp.where(odd, a, b), jnp.where(odd, b, a)

    return first, second, sort


def bits(count, first):
    out = []
    while first < count:
        out.append(first)
        first *= 2
    return out


def exchange(value, dims):
    n_row, n_col = lax.axis_size("row"), lax.axis_size("col")
    pairs = []
    for r in range(n_row):
        for c in range(n_col):
            dr, dc = dims[r & 1]
            pairs.append((r * n_col + c, (r ^ dr) * n_col + (c ^ dc)))
    return lax.ppermute(value, ("row", "col"), pairs)


def pack(value):
    return (value * (128.0 * lax.rsqrt(jnp.maximum(jnp.abs(value), 1e-36)))).astype(jnp.float16)


def unpack(got):
    root = got.astype(F32)
    return root * jnp.abs(root) * (1.0 / 128.0**2)


def local(field, near_kernel, contact, pillar_shift, wave_index, wave_form, wave_weight):
    rows, cols, sources, full = field.shape
    waves = wave_form.shape[0]
    n_row, n_col = lax.axis_size("row"), lax.axis_size("col")
    row_mod = Q * rows * n_row
    col_mod = Q * cols * n_col
    scale = math.sqrt(full // 2 / (waves * rows * n_row * cols * n_col))
    shift = jnp.swapaxes(pillar_shift, 1, 2)
    index = wave_index.T
    weight = wave_weight.reshape(1, -1)
    mine, other, form, form_other, trig, cells, mask = project(
        field.reshape(-1, full), shift, index, weight, contact, wave_form, row_mod, col_mod, scale
    )
    cells = cells.reshape(field.shape)
    total = mine + exchange(other, ((1, 0), (1, 0)))
    by_row = [(b, 0) for b in bits(n_row, 2)]
    by_col = [(0, b) for b in bits(n_col, 1)]
    steps = list(zip(by_row + by_col, by_row[::-1] + by_col[::-1]))
    tie = lax.optimization_barrier

    payload, here = tie((pack(total), cells))
    got = exchange(payload, steps[0])
    _, second, _ = paired(here[:, :1], here[:, cols - 1 :], "col")
    outer = second()
    total = total + unpack(got)

    payload, here = tie((pack(total), here))
    got = exchange(payload, steps[1])
    first, _, sort = paired(here[:, :1], here[:, cols - 1 :], "col")
    inner = first()
    out, sides = near_field((4,), (3, 5), mask, here, (), None, near_kernel)
    total = total + unpack(got)

    west, east = sort(inner, outer)
    payload, out = tie((pack(total), out))
    got = exchange(payload, steps[2])
    low = jnp.concatenate([west[:1], cells[:1], east[:1]], axis=1)
    high = jnp.concatenate([west[-1:], cells[-1:], east[-1:]], axis=1)
    first, second, sort = paired(low, high, "row")
    north, south = sort(first(), second())
    out, outer_held = near_field((3, 5), (0, 1, 2, 6, 7, 8), mask, cells, (west, east), sides, near_kernel, out)
    total = total + unpack(got)

    payload, out = tie((pack(total), out))
    got = exchange(payload, steps[3])
    halos = (west, east, north, south)
    (out,) = near_field((0, 1, 2, 6, 7, 8), (), mask, cells, halos, outer_held, near_kernel, out)
    total = total + unpack(got)
    for dims in steps[4:]:
        total = total + unpack(exchange(pack(total), dims))
    weighted, out = tie((total.astype(BF16), out))
    weighted_other = exchange(weighted, ((1, 0), (1, 0)))
    out = spread(trig, form, weighted, out, 0)
    out = spread(trig, form_other, weighted_other, out, 1)
    return out.reshape(field.shape)


def solution(mesh):
    placed = (
        P("row", "col", None, None),
        P(),
        P("row", "col", None),
        P("row", "col", None),
        P(),
        P(),
        P(),
    )
    return jax.shard_map(
        local, mesh=mesh, in_specs=placed, out_specs=P("row", "col", None, None), check_vma=False
    )
```

```python
import math

import jax
import jax.numpy as jnp
from jax import lax
from jax.experimental import pallas as pl
from jax.experimental.pallas import tpu as pltpu
from jax.sharding import PartitionSpec as P

Q = 16
LANES = 128
TILE = 256

bloch_row = 0.3
bloch_col = 0.17

F32 = jnp.float32
BF16 = jnp.bfloat16
NT = (((1,), (1,)), ((), ()))
HBM = pl.BlockSpec(memory_space=pltpu.MemorySpace.HBM)
VMEM = pl.BlockSpec(memory_space=pltpu.MemorySpace.VMEM)
SMEM = pl.BlockSpec(memory_space=pltpu.MemorySpace.SMEM)


def params(mib):
    return pltpu.CompilerParams(vmem_limit_bytes=mib << 20)


def cost(flops, size):
    return pl.CostEstimate(flops=flops, bytes_accessed=size, transcendentals=0)


def unit(turn):
    y = math.pi * turn
    z = y * y
    even = [(-1) ** k / math.factorial(2 * k) for k in range(8)]
    odd = [(-1) ** k / math.factorial(2 * k + 1) for k in range(8)]
    c = even[7]
    s = odd[7]
    for k in range(6, -1, -1):
        c = c * z + even[k]
        s = s * z + odd[k]
    s = s * y
    return 1.0 - 2.0 * (s * s), 2.0 * (s * c)


def fine(shift, lanes):
    rows, cols = shift.shape[0], shift.shape[2]
    first_row = lax.axis_index("row") * rows
    first_col = lax.axis_index("col") * cols
    spot = lax.broadcasted_iota(jnp.int32, (rows * cols, lanes), 0)
    fr = jnp.zeros(spot.shape, jnp.int32)
    fc = fr
    for p in range(rows * cols):
        r, c = p // cols, p % cols
        fr = jnp.where(spot == p, Q * (first_row + r) + shift[r, 0, c], fr)
        fc = jnp.where(spot == p, Q * (first_col + c) + shift[r, 1, c], fc)
    return fr, fc


def phases(fr, fc, index, row_mod, col_mod):
    turn_row = ((index[0:1] * fr) & (row_mod - 1)).astype(F32) * (1.0 / row_mod)
    turn_col = ((index[1:2] * fc) & (col_mod - 1)).astype(F32) * (1.0 / col_mod)
    drift = (bloch_row / row_mod) * fr.astype(F32) + (bloch_col / col_mod) * fc.astype(F32)
    turn = turn_row + turn_col + drift
    return unit(turn - jnp.round(turn))


def real_form(form, first, tile):
    re = form[0, first : first + tile, :]
    im = form[1, first : first + tile, :]
    upper = jnp.concatenate([re, -im], axis=1)
    lower = jnp.concatenate([im, re], axis=1)
    return jnp.concatenate([upper, lower], axis=0)


def project_body(x_hbm, shift_hbm, index_hbm, weight_hbm, contact_hbm, wave_hbm, kernel_hbm,
                 mine_ref, other_ref, mine_hbm, other_hbm, trig_ref, xs, mask_ref, middle_ref, sides_ref,
                 form_mine, form_other, form_sem, both, contact, shift, index_ref, weight_ref, g, sem, gsem,
                 *, tile, row_mod, col_mod, scale):
    waves = wave_hbm.shape[0]
    half = waves // 2
    width = wave_hbm.shape[2]
    n = shift.shape[0] * shift.shape[2]
    sources = x_hbm.shape[0] // n
    core = lax.axis_index("row") & 1
    small = [
        pltpu.make_async_copy(src, dst, sem.at[k])
        for k, (src, dst) in enumerate(
            (
                (shift_hbm, shift), (index_hbm, index_ref), (weight_hbm, weight_ref), (x_hbm, xs),
                (contact_hbm, contact), (kernel_hbm.at[4], middle_ref.at[0]),
                (kernel_hbm.at[3], sides_ref.at[0]), (kernel_hbm.at[5], sides_ref.at[1]),
            )
        )
    ]
    for c in small[:4]:
        c.start()
    steps = []
    for t in range(waves // tile):
        flip = 1 if t < waves // tile // 2 else 0
        inside = (t * tile) % half
        first = pl.multiple_of((core ^ flip) * half + inside, tile)
        pair = [pltpu.make_async_copy(wave_hbm.at[pl.ds(first, tile)], g.at[t], gsem.at[t])]
        for c in pair:
            c.start()
        steps.append((flip, inside, first, pair))
    for c in small[4:]:
        c.start()
    a = lax.broadcasted_iota(jnp.int32, (2 * LANES, 2 * LANES), 0)
    b = lax.broadcasted_iota(jnp.int32, (2 * LANES, 2 * LANES), 1)
    sort = jnp.where(b == jnp.where(a < LANES, 2 * a, 2 * (a - LANES) + 1), 1.0, 0.0).astype(BF16)
    for c in small[:3]:
        c.wait()
    fr, fc = fine(shift, tile)
    def unmix(t):
        flip, inside, first, pair = steps[t]
        if t == 0:
            pair[0].wait()
        if t == 1:
            for step in steps[1:]:
                step[3][0].wait()
        form = form_other if flip else form_mine
        for k in range(tile // LANES):
            mixed = g[t, k * LANES : (k + 1) * LANES].reshape(2 * LANES, width)
            d = jnp.dot(sort, mixed, preferred_element_type=F32).astype(BF16)
            at = slice(inside + k * LANES, inside + (k + 1) * LANES)
            form[0, at, :] = d[:LANES]
            form[1, at, :] = d[LANES:]

        copies = [
            pltpu.make_async_copy(
                form.at[k, pl.ds(inside, tile)],
                (other_hbm if flip else mine_hbm).at[k, pl.ds(inside, tile)],
                form_sem.at[t, k],
            )
            for k in range(2)
        ]
        for c in copies:
            c.start()
        return copies

    def multiply(t):
        flip, inside, first, pair = steps[t]
        form = form_other if flip else form_mine
        both[t % 2] = lax.dot_general(xs[...], real_form(form, inside, tile), NT, preferred_element_type=F32)

    def angles(t):
        flip, inside, first, pair = steps[t]
        at = pl.ds(first, tile)
        cos, sin = phases(fr, fc, index_ref[:, at], row_mod, col_mod)
        trig_ref[0, :, at] = cos
        trig_ref[1, :, at] = sin

    def add(t):
        flip, inside, first, pair = steps[t]
        at = pl.ds(first, tile)
        ar = jnp.zeros((sources, tile), F32)
        ai = ar
        for p in range(n):
            here = slice(p * sources, (p + 1) * sources)
            u, v = both[t % 2, here, :tile], both[t % 2, here, tile:]
            cp, sp = trig_ref[0, p : p + 1, at], trig_ref[1, p : p + 1, at]
            ar = ar + (cp * u - sp * v)
            ai = ai + (cp * v + sp * u)
        s = scale * weight_ref[:, at]
        ar = ar * s
        ai = ai * s
        out = other_ref if flip else mine_ref
        for k in range(tile // LANES):
            out[inside // LANES + k, 0] = ar[:, LANES * k : LANES * (k + 1)]
            out[inside // LANES + k, 1] = ai[:, LANES * k : LANES * (k + 1)]

    count = len(steps)
    angles(0)
    stores = unmix(0)
    small[3].wait()
    for t in range(count):
        if t + 1 < count:
            stores += unmix(t + 1)
        multiply(t)
        if t + 1 < count:
            angles(t + 1)
        if t > 0:
            add(t - 1)
    add(count - 1)
    for c in small[4:] + stores:
        c.wait()
    cols = shift.shape[2]
    for o in range(mask_ref.shape[0]):
        for p in range(n):
            chosen = jnp.full((1, LANES), contact[p // cols, p % cols, o], jnp.int32)
            mask_ref[o, p : p + 1, :] = chosen.astype(F32)


def in_hbm(*arrays):
    return [pltpu.with_memory_space_constraint(a, pltpu.MemorySpace.HBM) for a in arrays]


def project(x, shift, index, weight, contact, wave_form, near_kernel, row_mod, col_mod, scale, tile=TILE):
    waves, _, width = wave_form.shape
    n = shift.shape[0] * shift.shape[2]
    sources = x.shape[0] // n
    half = pltpu.VMEM((waves // 2 // LANES, 2, sources, LANES), F32)

    form = pltpu.HBM((2, waves // 2, width), BF16)

    def body(*refs):
        project_body(*refs, tile=tile, row_mod=row_mod, col_mod=col_mod, scale=scale)

    return pl.pallas_call(
        body,
        in_specs=[HBM] * 7,
        out_specs=[VMEM] * 2 + [HBM] * 2 + [VMEM] * 5,
        out_shape=[
            half,
            half,
            form,
            form,
            pltpu.VMEM((2, n, waves), F32),
            pltpu.VMEM(x.shape, BF16),
            pltpu.VMEM((contact.shape[2], n, LANES), F32),
            pltpu.VMEM((1,) + near_kernel.shape[1:], BF16),
            pltpu.VMEM((2,) + near_kernel.shape[1:], BF16),
        ],
        scratch_shapes=[
            pltpu.VMEM((2, waves // 2, width), BF16),
            pltpu.VMEM((2, waves // 2, width), BF16),
            pltpu.SemaphoreType.DMA((waves // tile, 2)),
            pltpu.VMEM((2, x.shape[0], 2 * tile), F32),
            pltpu.SMEM(contact.shape, jnp.int32),
            pltpu.SMEM(shift.shape, jnp.int32),
            pltpu.VMEM(index.shape, jnp.int32),
            pltpu.VMEM(weight.shape, F32),
            pltpu.VMEM((waves // tile, tile, 2, width), BF16),
            pltpu.SemaphoreType.DMA((8,)),
            pltpu.SemaphoreType.DMA((waves // tile,)),
        ],
        compiler_params=params(24),
        cost_estimate=cost(8 * x.shape[0] * width * waves, 5 << 20),
        name="project",
    )(*in_hbm(x, shift, index, weight, contact, wave_form, near_kernel))


def spread_body(trig_ref, form_ref, coeff_ref, base_ref, out_ref, lhs, *, flip, tile):
    waves = trig_ref.shape[2]
    half = waves // 2
    n = trig_ref.shape[1]
    sources = coeff_ref.shape[2]
    core = (lax.axis_index("row") & 1) ^ flip
    for t in range(half // tile):
        at = pl.ds(pl.multiple_of(core * half + t * tile, tile), tile)
        cos, sin = trig_ref[0, :, at], trig_ref[1, :, at]
        groups = range(t * tile // LANES, (t + 1) * tile // LANES)
        wr = jnp.concatenate([coeff_ref[k, 0].astype(F32) for k in groups], axis=1)
        wi = jnp.concatenate([coeff_ref[k, 1].astype(F32) for k in groups], axis=1)
        for p in range(n):
            cp, sp = cos[p : p + 1], sin[p : p + 1]
            here = slice(p * sources, (p + 1) * sources)
            lhs[t, here, :tile] = (cp * wr + sp * wi).astype(BF16)
            lhs[t, here, tile:] = (cp * wi - sp * wr).astype(BF16)
        src = base_ref if t == 0 else out_ref
        w = real_form(form_ref, t * tile, tile)
        out_ref[...] = src[...] + jnp.dot(lhs[t], w, preferred_element_type=F32)


def spread(trig, form, coeff, base, flip, tile=TILE):
    half = trig.shape[2] // 2

    def body(*refs):
        spread_body(*refs, flip=flip, tile=tile)

    return pl.pallas_call(
        body,
        in_specs=[VMEM] * 4,
        out_specs=VMEM,
        out_shape=jax.ShapeDtypeStruct(base.shape, F32),
        scratch_shapes=[pltpu.VMEM((half // tile, base.shape[0], 2 * tile), BF16)],
        compiler_params=params(24),
        cost_estimate=cost(4 * base.shape[0] * base.shape[1] * half, 5 << 20),
        name="spread",
    )(trig, form, coeff, base)


def near_body(*refs, offsets, coming, halo, after):
    mask_ref, x = refs[:2]
    halos = refs[2 : 2 + halo]
    held, refs = refs[2 + halo], refs[3 + halo :]
    if coming:
        kernel_hbm, refs = refs[0], refs[1:]
    if after:
        base_ref, refs = refs[0], refs[1:]
    out_ref, refs = refs[0], refs[1:]
    copies = []
    if coming:
        copies = [
            pltpu.make_async_copy(kernel_hbm.at[o], refs[0].at[k], refs[2].at[k]) for k, o in enumerate(coming)
        ]
        for c in copies:
            c.start()
        refs = refs[1:]
    lhs = refs[0]
    rows, cols, sources, full = x.shape
    classes = held.shape[1]

    def block(r, c):
        if r < 0:
            return halos[2][0, c + 1]
        if r >= rows:
            return halos[3][0, c + 1]
        if c < 0:
            return halos[0][r, 0]
        if c >= cols:
            return halos[1][r, 0]
        return x[r, c]

    def gather(k):
        o = offsets[k]
        for p in range(rows * cols):
            r, c = p // cols, p % cols
            here = slice(p * sources, (p + 1) * sources)
            xb = block(r + o // 3 - 1, c + o % 3 - 1)
            m = jnp.broadcast_to(mask_ref[o, p : p + 1, :], (sources, LANES)).astype(BF16)
            second = xb * jnp.concatenate([m] * (full // LANES), axis=1)
            lhs[k % 2, here, :full] = xb - second
            lhs[k % 2, here, full:] = second

    for k, o in enumerate(offsets):
        gather(k)
        upper, lower = [], []
        for v in range(classes):
            re, im = held[k, v, 0], held[k, v, 1]
            upper += [re, -im]
            lower += [im, re]
        w = jnp.concatenate([jnp.concatenate(upper, axis=1), jnp.concatenate(lower, axis=1)], axis=0)
        product = lax.dot_general(lhs[k % 2], w, NT, preferred_element_type=F32)
        if k == 0 and not after:
            out_ref[...] = product
        else:
            out_ref[...] = (base_ref if k == 0 else out_ref)[...] + product


    for c in copies:
        c.wait()


def near_field(offsets, coming, mask, x, halos, held, kernel, base=None):
    rows, cols, sources, full = x.shape
    m = rows * cols * sources
    classes = kernel.shape[1]
    after = base is not None

    def body(*refs):
        near_body(*refs, offsets=offsets, coming=coming, halo=len(halos), after=after)

    operands = [mask, x, *halos, held]
    specs = [VMEM] * len(operands)
    out = [pltpu.VMEM((m, full), F32)]
    scratch = [pltpu.VMEM((2, m, classes * full), BF16)]
    if coming:
        operands += in_hbm(kernel)
        specs += [HBM]
        out += [pltpu.VMEM((len(coming),) + kernel.shape[1:], BF16)]
        scratch += [pltpu.SemaphoreType.DMA((len(coming),))]
    return pl.pallas_call(
        body,
        in_specs=specs + [VMEM] * after,
        out_specs=[VMEM] * len(out),
        out_shape=out,
        scratch_shapes=scratch,
        compiler_params=params(24),
        cost_estimate=cost(2 * len(offsets) * classes * m * full * full, 4 << 20),
        name="near",
    )(*operands, *[base] * after)


def paired(low, high, axis):
    count = lax.axis_size(axis)
    odd = (lax.axis_index(axis) & 1) == 1
    inner = [(i, i ^ 1) for i in range(count)]
    outer = [(i, (i + 1 if i & 1 else i - 1) % count) for i in range(count)]

    def first():
        return lax.ppermute(jnp.where(odd, low, high), axis, inner)

    def second():
        return lax.ppermute(jnp.where(odd, high, low), axis, outer)

    def sort(a, b):
        return jnp.where(odd, a, b), jnp.where(odd, b, a)

    return first, second, sort


def bits(count, first):
    out = []
    while first < count:
        out.append(first)
        first *= 2
    return out


def exchange(value, dims):
    n_row, n_col = lax.axis_size("row"), lax.axis_size("col")
    pairs = []
    for r in range(n_row):
        for c in range(n_col):
            dr, dc = dims[r & 1]
            pairs.append((r * n_col + c, (r ^ dr) * n_col + (c ^ dc)))
    return lax.ppermute(value, ("row", "col"), pairs)


def pack(value):
    return (value * (128.0 * lax.rsqrt(jnp.maximum(jnp.abs(value), 1e-36)))).astype(jnp.float16)


def unpack(got):
    root = got.astype(F32)
    return root * jnp.abs(root) * (1.0 / 128.0**2)


def local(field, near_kernel, contact, pillar_shift, wave_index, wave_form, wave_weight):
    rows, cols, sources, full = field.shape
    waves = wave_form.shape[0]
    n_row, n_col = lax.axis_size("row"), lax.axis_size("col")
    row_mod = Q * rows * n_row
    col_mod = Q * cols * n_col
    scale = math.sqrt(full // 2 / (waves * rows * n_row * cols * n_col))
    shift = jnp.swapaxes(pillar_shift, 1, 2)
    index = wave_index.T
    weight = wave_weight.reshape(1, -1)
    mine, other, form, form_other, trig, cells, mask, middle, sides = project(
        field.reshape(-1, full), shift, index, weight, contact, wave_form, near_kernel, row_mod, col_mod, scale
    )
    cells = cells.reshape(field.shape)
    total = mine + exchange(other, ((1, 0), (1, 0)))
    by_row = [(b, 0) for b in bits(n_row, 2)]
    by_col = [(0, b) for b in bits(n_col, 1)]
    steps = list(zip(by_row + by_col, by_row[::-1] + by_col[::-1]))
    tie = lax.optimization_barrier

    payload, here = tie((pack(total), cells))
    got = exchange(payload, steps[0])
    _, second, _ = paired(here[:, :1], here[:, cols - 1 :], "col")
    outer = second()
    total = total + unpack(got)

    payload, here = tie((pack(total), here))
    got = exchange(payload, steps[1])
    first, _, sort = paired(here[:, :1], here[:, cols - 1 :], "col")
    inner = first()
    out, outer_held = near_field((4,), (0, 1, 2, 6, 7, 8), mask, here, (), middle, near_kernel)
    total = total + unpack(got)

    west, east = sort(inner, outer)
    payload, out = tie((pack(total), out))
    got = exchange(payload, steps[2])
    low = jnp.concatenate([west[:1], cells[:1], east[:1]], axis=1)
    high = jnp.concatenate([west[-1:], cells[-1:], east[-1:]], axis=1)
    first, second, sort = paired(low, high, "row")
    north, south = sort(first(), second())
    (out,) = near_field((3, 5), (), mask, cells, (west, east), sides, near_kernel, out)
    total = total + unpack(got)

    payload, out = tie((pack(total), out))
    got = exchange(payload, steps[3])
    halos = (west, east, north, south)
    (out,) = near_field((0, 1, 2, 6, 7, 8), (), mask, cells, halos, outer_held, near_kernel, out)
    total = total + unpack(got)
    for dims in steps[4:]:
        total = total + unpack(exchange(pack(total), dims))
    weighted, out = tie((total.astype(BF16), out))
    weighted_other = exchange(weighted, ((1, 0), (1, 0)))
    out = spread(trig, form, weighted, out, 0)
    out = spread(trig, form_other, weighted_other, out, 1)
    return out.reshape(field.shape)


def solution(mesh):
    placed = (
        P("row", "col", None, None),
        P(),
        P("row", "col", None),
        P("row", "col", None),
        P(),
        P(),
        P(),
    )
    return jax.shard_map(
        local, mesh=mesh, in_specs=placed, out_specs=P("row", "col", None, None), check_vma=False
    )
```

```python
import math

import jax
import jax.numpy as jnp
from jax import lax
from jax.experimental import pallas as pl
from jax.experimental.pallas import tpu as pltpu
from jax.sharding import PartitionSpec as P

Q = 16
LANES = 128
TILE = 256

bloch_row = 0.3
bloch_col = 0.17

F32 = jnp.float32
BF16 = jnp.bfloat16
NT = (((1,), (1,)), ((), ()))
HBM = pl.BlockSpec(memory_space=pltpu.MemorySpace.HBM)
VMEM = pl.BlockSpec(memory_space=pltpu.MemorySpace.VMEM)
SMEM = pl.BlockSpec(memory_space=pltpu.MemorySpace.SMEM)


def params(mib):
    return pltpu.CompilerParams(vmem_limit_bytes=mib << 20)


def cost(flops, size):
    return pl.CostEstimate(flops=flops, bytes_accessed=size, transcendentals=0)


def unit(turn):
    y = math.pi * turn
    z = y * y
    even = [(-1) ** k / math.factorial(2 * k) for k in range(8)]
    odd = [(-1) ** k / math.factorial(2 * k + 1) for k in range(8)]
    c = even[7]
    s = odd[7]
    for k in range(6, -1, -1):
        c = c * z + even[k]
        s = s * z + odd[k]
    s = s * y
    return 1.0 - 2.0 * (s * s), 2.0 * (s * c)


def fine(shift, lanes):
    rows, cols = shift.shape[0], shift.shape[2]
    first_row = lax.axis_index("row") * rows
    first_col = lax.axis_index("col") * cols
    spot = lax.broadcasted_iota(jnp.int32, (rows * cols, lanes), 0)
    fr = jnp.zeros(spot.shape, jnp.int32)
    fc = fr
    for p in range(rows * cols):
        r, c = p // cols, p % cols
        fr = jnp.where(spot == p, Q * (first_row + r) + shift[r, 0, c], fr)
        fc = jnp.where(spot == p, Q * (first_col + c) + shift[r, 1, c], fc)
    return fr, fc


def phases(fr, fc, index, row_mod, col_mod):
    turn_row = ((index[0:1] * fr) & (row_mod - 1)).astype(F32) * (1.0 / row_mod)
    turn_col = ((index[1:2] * fc) & (col_mod - 1)).astype(F32) * (1.0 / col_mod)
    drift = (bloch_row / row_mod) * fr.astype(F32) + (bloch_col / col_mod) * fc.astype(F32)
    turn = turn_row + turn_col + drift
    return unit(turn - jnp.round(turn))


def real_form(form, first, tile):
    re = form[0, first : first + tile, :]
    im = form[1, first : first + tile, :]
    upper = jnp.concatenate([re, -im], axis=1)
    lower = jnp.concatenate([im, re], axis=1)
    return jnp.concatenate([upper, lower], axis=0)


def project_body(x_hbm, shift_hbm, index_hbm, weight_hbm, contact_hbm, wave_hbm, kernel_hbm,
                 mine_ref, other_ref, mine_hbm, other_hbm, trig_ref, xs, mask_ref, middle_ref, sides_ref,
                 form_mine, form_other, form_sem, both, contact, shift, index_ref, weight_ref, g, sem, gsem,
                 *, tile, row_mod, col_mod, scale):
    waves = wave_hbm.shape[0]
    half = waves // 2
    width = wave_hbm.shape[2]
    n = shift.shape[0] * shift.shape[2]
    sources = x_hbm.shape[0] // n
    core = lax.axis_index("row") & 1
    small = [
        pltpu.make_async_copy(src, dst, sem.at[k])
        for k, (src, dst) in enumerate(
            (
                (shift_hbm, shift), (index_hbm, index_ref), (weight_hbm, weight_ref), (x_hbm, xs),
                (contact_hbm, contact), (kernel_hbm.at[4], middle_ref.at[0]),
                (kernel_hbm.at[3], sides_ref.at[0]), (kernel_hbm.at[5], sides_ref.at[1]),
            )
        )
    ]
    for c in small[:4]:
        c.start()
    steps = []
    for t in range(waves // tile):
        flip = 1 if t < waves // tile // 2 else 0
        inside = (t * tile) % half
        first = pl.multiple_of((core ^ flip) * half + inside, tile)
        pair = [pltpu.make_async_copy(wave_hbm.at[pl.ds(first, tile)], g.at[t], gsem.at[t])]
        for c in pair:
            c.start()
        steps.append((flip, inside, first, pair))
    for c in small[4:]:
        c.start()
    a = lax.broadcasted_iota(jnp.int32, (2 * LANES, 2 * LANES), 0)
    b = lax.broadcasted_iota(jnp.int32, (2 * LANES, 2 * LANES), 1)
    sort = jnp.where(b == jnp.where(a < LANES, 2 * a, 2 * (a - LANES) + 1), 1.0, 0.0).astype(BF16)
    for c in small[:3]:
        c.wait()
    fr, fc = fine(shift, tile)
    def unmix(t):
        flip, inside, first, pair = steps[t]
        if t == 0:
            pair[0].wait()
        if t == 1:
            for step in steps[1:]:
                step[3][0].wait()
        form = form_other if flip else form_mine
        for k in range(tile // LANES):
            mixed = g[t, k * LANES : (k + 1) * LANES].reshape(2 * LANES, width)
            d = jnp.dot(sort, mixed, preferred_element_type=F32).astype(BF16)
            at = slice(inside + k * LANES, inside + (k + 1) * LANES)
            form[0, at, :] = d[:LANES]
            form[1, at, :] = d[LANES:]

        copies = [
            pltpu.make_async_copy(
                form.at[k, pl.ds(inside, tile)],
                (other_hbm if flip else mine_hbm).at[k, pl.ds(inside, tile)],
                form_sem.at[t, k],
            )
            for k in range(2)
        ]
        for c in copies:
            c.start()
        return copies

    def multiply(t):
        flip, inside, first, pair = steps[t]
        form = form_other if flip else form_mine
        both[t % 2] = lax.dot_general(xs[...], real_form(form, inside, tile), NT, preferred_element_type=F32)

    def angles(t):
        flip, inside, first, pair = steps[t]
        at = pl.ds(first, tile)
        cos, sin = phases(fr, fc, index_ref[:, at], row_mod, col_mod)
        trig_ref[0, :, at] = cos
        trig_ref[1, :, at] = sin

    def add(t):
        flip, inside, first, pair = steps[t]
        at = pl.ds(first, tile)
        ar = jnp.zeros((sources, tile), F32)
        ai = ar
        for p in range(n):
            here = slice(p * sources, (p + 1) * sources)
            u, v = both[t % 2, here, :tile], both[t % 2, here, tile:]
            cp, sp = trig_ref[0, p : p + 1, at], trig_ref[1, p : p + 1, at]
            ar = ar + (cp * u - sp * v)
            ai = ai + (cp * v + sp * u)
        s = scale * weight_ref[:, at]
        ar = ar * s
        ai = ai * s
        out = other_ref if flip else mine_ref
        for k in range(tile // LANES):
            out[inside // LANES + k, 0] = ar[:, LANES * k : LANES * (k + 1)]
            out[inside // LANES + k, 1] = ai[:, LANES * k : LANES * (k + 1)]

    count = len(steps)
    angles(0)
    stores = unmix(0)
    small[3].wait()
    for t in range(count):
        if t + 1 < count:
            stores += unmix(t + 1)
        multiply(t)
        if t + 1 < count:
            angles(t + 1)
        if t > 0:
            add(t - 1)
    add(count - 1)
    small[4].wait()
    cols = shift.shape[2]
    for o in range(mask_ref.shape[0]):
        for p in range(n):
            chosen = jnp.full((1, LANES), contact[p // cols, p % cols, o], jnp.int32)
            mask_ref[o, p : p + 1, :] = chosen.astype(F32)
    for c in small[5:] + stores:
        c.wait()


def in_hbm(*arrays):
    return [pltpu.with_memory_space_constraint(a, pltpu.MemorySpace.HBM) for a in arrays]


def project(x, shift, index, weight, contact, wave_form, near_kernel, row_mod, col_mod, scale, tile=TILE):
    waves, _, width = wave_form.shape
    n = shift.shape[0] * shift.shape[2]
    sources = x.shape[0] // n
    half = pltpu.VMEM((waves // 2 // LANES, 2, sources, LANES), F32)

    form = pltpu.HBM((2, waves // 2, width), BF16)

    def body(*refs):
        project_body(*refs, tile=tile, row_mod=row_mod, col_mod=col_mod, scale=scale)

    return pl.pallas_call(
        body,
        in_specs=[HBM] * 7,
        out_specs=[VMEM] * 2 + [HBM] * 2 + [VMEM] * 5,
        out_shape=[
            half,
            half,
            form,
            form,
            pltpu.VMEM((2, n, waves), F32),
            pltpu.VMEM(x.shape, BF16),
            pltpu.VMEM((contact.shape[2], n, LANES), F32),
            pltpu.VMEM((1,) + near_kernel.shape[1:], BF16),
            pltpu.VMEM((2,) + near_kernel.shape[1:], BF16),
        ],
        scratch_shapes=[
            pltpu.VMEM((2, waves // 2, width), BF16),
            pltpu.VMEM((2, waves // 2, width), BF16),
            pltpu.SemaphoreType.DMA((waves // tile, 2)),
            pltpu.VMEM((2, x.shape[0], 2 * tile), F32),
            pltpu.SMEM(contact.shape, jnp.int32),
            pltpu.SMEM(shift.shape, jnp.int32),
            pltpu.VMEM(index.shape, jnp.int32),
            pltpu.VMEM(weight.shape, F32),
            pltpu.VMEM((waves // tile, tile, 2, width), BF16),
            pltpu.SemaphoreType.DMA((8,)),
            pltpu.SemaphoreType.DMA((waves // tile,)),
        ],
        compiler_params=params(24),
        cost_estimate=cost(8 * x.shape[0] * width * waves, 5 << 20),
        name="project",
    )(*in_hbm(x, shift, index, weight, contact, wave_form, near_kernel))


def spread_body(trig_ref, form_ref, coeff_ref, base_ref, out_ref, lhs, *, flip, tile):
    waves = trig_ref.shape[2]
    half = waves // 2
    n = trig_ref.shape[1]
    sources = coeff_ref.shape[2]
    core = (lax.axis_index("row") & 1) ^ flip
    for t in range(half // tile):
        at = pl.ds(pl.multiple_of(core * half + t * tile, tile), tile)
        cos, sin = trig_ref[0, :, at], trig_ref[1, :, at]
        groups = range(t * tile // LANES, (t + 1) * tile // LANES)
        wr = jnp.concatenate([coeff_ref[k, 0].astype(F32) for k in groups], axis=1)
        wi = jnp.concatenate([coeff_ref[k, 1].astype(F32) for k in groups], axis=1)
        for p in range(n):
            cp, sp = cos[p : p + 1], sin[p : p + 1]
            here = slice(p * sources, (p + 1) * sources)
            lhs[t, here, :tile] = (cp * wr + sp * wi).astype(BF16)
            lhs[t, here, tile:] = (cp * wi - sp * wr).astype(BF16)
        src = base_ref if t == 0 else out_ref
        w = real_form(form_ref, t * tile, tile)
        out_ref[...] = src[...] + jnp.dot(lhs[t], w, preferred_element_type=F32)


def spread(trig, form, coeff, base, flip, tile=TILE):
    half = trig.shape[2] // 2

    def body(*refs):
        spread_body(*refs, flip=flip, tile=tile)

    return pl.pallas_call(
        body,
        in_specs=[VMEM] * 4,
        out_specs=VMEM,
        out_shape=jax.ShapeDtypeStruct(base.shape, F32),
        scratch_shapes=[pltpu.VMEM((half // tile, base.shape[0], 2 * tile), BF16)],
        compiler_params=params(24),
        cost_estimate=cost(4 * base.shape[0] * base.shape[1] * half, 5 << 20),
        name="spread",
    )(trig, form, coeff, base)


def near_body(*refs, offsets, coming, halo, after):
    mask_ref, x = refs[:2]
    halos = refs[2 : 2 + halo]
    held, refs = refs[2 + halo], refs[3 + halo :]
    if coming:
        kernel_hbm, refs = refs[0], refs[1:]
    if after:
        base_ref, refs = refs[0], refs[1:]
    out_ref, refs = refs[0], refs[1:]
    copies = []
    if coming:
        copies = [
            pltpu.make_async_copy(kernel_hbm.at[o], refs[0].at[k], refs[2].at[k]) for k, o in enumerate(coming)
        ]
        for c in copies:
            c.start()
        refs = refs[1:]
    lhs = refs[0]
    rows, cols, sources, full = x.shape
    classes = held.shape[1]

    def block(r, c):
        if r < 0:
            return halos[2][0, c + 1]
        if r >= rows:
            return halos[3][0, c + 1]
        if c < 0:
            return halos[0][r, 0]
        if c >= cols:
            return halos[1][r, 0]
        return x[r, c]

    def gather(k):
        o = offsets[k]
        for p in range(rows * cols):
            r, c = p // cols, p % cols
            here = slice(p * sources, (p + 1) * sources)
            xb = block(r + o // 3 - 1, c + o % 3 - 1)
            m = jnp.broadcast_to(mask_ref[o, p : p + 1, :], (sources, LANES)).astype(BF16)
            second = xb * jnp.concatenate([m] * (full // LANES), axis=1)
            lhs[k % 2, here, :full] = xb - second
            lhs[k % 2, here, full:] = second

    for k, o in enumerate(offsets):
        gather(k)
        upper, lower = [], []
        for v in range(classes):
            re, im = held[k, v, 0], held[k, v, 1]
            upper += [re, -im]
            lower += [im, re]
        w = jnp.concatenate([jnp.concatenate(upper, axis=1), jnp.concatenate(lower, axis=1)], axis=0)
        product = lax.dot_general(lhs[k % 2], w, NT, preferred_element_type=F32)
        if k == 0 and not after:
            out_ref[...] = product
        else:
            out_ref[...] = (base_ref if k == 0 else out_ref)[...] + product


    for c in copies:
        c.wait()


def near_field(offsets, coming, mask, x, halos, held, kernel, base=None):
    rows, cols, sources, full = x.shape
    m = rows * cols * sources
    classes = kernel.shape[1]
    after = base is not None

    def body(*refs):
        near_body(*refs, offsets=offsets, coming=coming, halo=len(halos), after=after)

    operands = [mask, x, *halos, held]
    specs = [VMEM] * len(operands)
    out = [pltpu.VMEM((m, full), F32)]
    scratch = [pltpu.VMEM((2, m, classes * full), BF16)]
    if coming:
        operands += in_hbm(kernel)
        specs += [HBM]
        out += [pltpu.VMEM((len(coming),) + kernel.shape[1:], BF16)]
        scratch += [pltpu.SemaphoreType.DMA((len(coming),))]
    return pl.pallas_call(
        body,
        in_specs=specs + [VMEM] * after,
        out_specs=[VMEM] * len(out),
        out_shape=out,
        scratch_shapes=scratch,
        compiler_params=params(24),
        cost_estimate=cost(2 * len(offsets) * classes * m * full * full, 4 << 20),
        name="near",
    )(*operands, *[base] * after)


def paired(low, high, axis):
    count = lax.axis_size(axis)
    odd = (lax.axis_index(axis) & 1) == 1
    inner = [(i, i ^ 1) for i in range(count)]
    outer = [(i, (i + 1 if i & 1 else i - 1) % count) for i in range(count)]

    def first():
        return lax.ppermute(jnp.where(odd, low, high), axis, inner)

    def second():
        return lax.ppermute(jnp.where(odd, high, low), axis, outer)

    def sort(a, b):
        return jnp.where(odd, a, b), jnp.where(odd, b, a)

    return first, second, sort


def bits(count, first):
    out = []
    while first < count:
        out.append(first)
        first *= 2
    return out


def exchange(value, dims):
    n_row, n_col = lax.axis_size("row"), lax.axis_size("col")
    pairs = []
    for r in range(n_row):
        for c in range(n_col):
            dr, dc = dims[r & 1]
            pairs.append((r * n_col + c, (r ^ dr) * n_col + (c ^ dc)))
    return lax.ppermute(value, ("row", "col"), pairs)


def pack(value):
    return (value * (128.0 * lax.rsqrt(jnp.maximum(jnp.abs(value), 1e-36)))).astype(jnp.float16)


def unpack(got):
    root = got.astype(F32)
    return root * jnp.abs(root) * (1.0 / 128.0**2)


def local(field, near_kernel, contact, pillar_shift, wave_index, wave_form, wave_weight):
    rows, cols, sources, full = field.shape
    waves = wave_form.shape[0]
    n_row, n_col = lax.axis_size("row"), lax.axis_size("col")
    row_mod = Q * rows * n_row
    col_mod = Q * cols * n_col
    scale = math.sqrt(full // 2 / (waves * rows * n_row * cols * n_col))
    shift = jnp.swapaxes(pillar_shift, 1, 2)
    index = wave_index.T
    weight = wave_weight.reshape(1, -1)
    mine, other, form, form_other, trig, cells, mask, middle, sides = project(
        field.reshape(-1, full), shift, index, weight, contact, wave_form, near_kernel, row_mod, col_mod, scale
    )
    cells = cells.reshape(field.shape)
    total = mine + exchange(other, ((1, 0), (1, 0)))
    by_row = [(b, 0) for b in bits(n_row, 2)]
    by_col = [(0, b) for b in bits(n_col, 1)]
    steps = list(zip(by_row + by_col, by_row[::-1] + by_col[::-1]))
    tie = lax.optimization_barrier

    payload, here = tie((pack(total), cells))
    got = exchange(payload, steps[0])
    _, second, _ = paired(here[:, :1], here[:, cols - 1 :], "col")
    outer = second()
    total = total + unpack(got)

    payload, here = tie((pack(total), here))
    got = exchange(payload, steps[1])
    first, _, sort = paired(here[:, :1], here[:, cols - 1 :], "col")
    inner = first()
    out, outer_held = near_field((4,), (0, 1, 2, 6, 7, 8), mask, here, (), middle, near_kernel)
    total = total + unpack(got)

    west, east = sort(inner, outer)
    payload, out = tie((pack(total), out))
    got = exchange(payload, steps[2])
    low = jnp.concatenate([west[:1], cells[:1], east[:1]], axis=1)
    high = jnp.concatenate([west[-1:], cells[-1:], east[-1:]], axis=1)
    first, second, sort = paired(low, high, "row")
    north, south = sort(first(), second())
    (out,) = near_field((3, 5), (), mask, cells, (west, east), sides, near_kernel, out)
    total = total + unpack(got)

    payload, out = tie((pack(total), out))
    got = exchange(payload, steps[3])
    halos = (west, east, north, south)
    (out,) = near_field((0, 1, 2, 6, 7, 8), (), mask, cells, halos, outer_held, near_kernel, out)
    total = total + unpack(got)
    for dims in steps[4:]:
        total = total + unpack(exchange(pack(total), dims))
    weighted, out = tie((total.astype(BF16), out))
    weighted_other = exchange(weighted, ((1, 0), (1, 0)))
    out = spread(trig, form, weighted, out, 0)
    out = spread(trig, form_other, weighted_other, out, 1)
    return out.reshape(field.shape)


def solution(mesh):
    placed = (
        P("row", "col", None, None),
        P(),
        P("row", "col", None),
        P("row", "col", None),
        P(),
        P(),
        P(),
    )
    return jax.shard_map(
        local, mesh=mesh, in_specs=placed, out_specs=P("row", "col", None, None), check_vma=False
    )
```
